32 devices in a mesh: ctx: 8 (over y, x, core), ch: 4 (over z).
Axes of the slice: x: 2, y: 2, z: 4, core: 2. Of those that a mesh axis runs over, the one named last changes fastest.
Arguments:
- stream: bfloat16 [4096, 4096], P('ctx', 'ch'), may hold values from -900 to 900
- key_gate: bfloat16 [4096, 4096], P('ctx', 'ch'), may hold values from -6 to 6
- query_gate: bfloat16 [4096, 4096], P('ctx', 'ch'), may hold values from -6 to 6
- grad_output: bfloat16 [4096, 4096], P('ctx', 'ch'), may hold values from -50 to 50
- norm_gain: float32 [4096], P('ch'), may hold values from 0.1 to 1.9
- residue: float32 [4096, 16], P('ch'), may hold values from -0.5 to 0.5
- log_rate: float32 [4096, 16], P('ch'), may hold values from -14 to -2.9
Outputs:
- output: bfloat16 [4096, 4096], P('ctx', 'ch')
- grad_stream: bfloat16 [4096, 4096], P('ctx', 'ch')
- grad_key: bfloat16 [4096, 4096], P('ctx', 'ch')
- grad_query: bfloat16 [4096, 4096], P('ctx', 'ch')
- grad_gain: float32 [4096], P('ch')
- grad_residue: float32 [4096, 16], P('ch')
- grad_rate: float32 [4096, 16], P('ch')
The draws below stay inside these ranges and needn't reach their ends.
All inputs are finite; a program needn't handle non-finite values.
Results may differ from the reference program's by a relative error of at most 0.008.
Values sent between devices are 32-bit elements; how exact they have to be, the bound alone decides.
A program may use at most 128 MiB of HBM per device.

```python
import math
import jax
import jax.numpy as jnp
from jax import lax

D = 4096
MODES = 16
SEQ = 4096


def draw_stream(key, part):
    keys = jax.random.split(key, 3)
    base = jnp.clip(jax.random.normal(keys[0], (SEQ, D), jnp.float32), -6.0, 6.0)
    row_log = jax.random.uniform(keys[1], (SEQ, 1), jnp.float32, 0.0, math.log(10.0))
    col_log = math.log(10.0) * jnp.arange(D, dtype=jnp.float32)[None, :] / D
    col_log = col_log + jax.random.uniform(keys[2], (1, D), jnp.float32, -0.25, 0.25)
    return (base * jnp.exp(row_log) * jnp.exp(col_log)).astype(jnp.bfloat16)


def draw_grad_output(key, part):
    keys = jax.random.split(key, 2)
    position = jnp.arange(SEQ, dtype=jnp.float32)[:, None] / SEQ
    base = jnp.clip(jax.random.normal(keys[0], (SEQ, D), jnp.float32), -6.0, 6.0)
    rising = math.log(3.0) * position
    jitter = jax.random.uniform(keys[1], (SEQ, 1), jnp.float32, -0.3, 0.3)
    return (base * jnp.exp(rising + jitter)).astype(jnp.bfloat16)


def mode_draw(key):
    keys = jax.random.split(jax.random.fold_in(key, 11), 5)
    shape = (D, MODES)
    picker = jax.random.uniform(keys[0], shape, jnp.float32)
    slow = jnp.exp(jax.random.uniform(keys[1], shape, jnp.float32, math.log(0.1 / SEQ), math.log(2.0 / SEQ)))
    middle = jnp.exp(jax.random.uniform(keys[2], shape, jnp.float32, math.log(2.0 / SEQ), math.log(1.0 / 50.0)))
    fast = jnp.exp(jax.random.uniform(keys[3], shape, jnp.float32, math.log(1.0 / 50.0), math.log(1.0 / 20.0)))
    decay_rate = jnp.where(picker < 0.5, slow, jnp.where(picker < 0.75, middle, fast))
    factor = jnp.clip(jax.random.normal(keys[4], shape, jnp.float32), -6.0, 6.0)
    residue = factor * jnp.sqrt((2.0 * decay_rate + 2.0 / SEQ) / MODES)
    return (jnp.log(decay_rate), residue)


def draw_residue(key, part):
    return mode_draw(key)[1].astype(jnp.float32)


def draw_log_rate(key, part):
    return mode_draw(key)[0].astype(jnp.float32)


def block_scale(key, dims, cuts, least, high):
    level, own = 1.0, jax.random.fold_in(key, 6)
    for axis_at, blocks in cuts:
        steps = jnp.exp(jax.random.uniform(jax.random.fold_in(own, axis_at), (blocks,), jnp.float32, least / len(cuts), high / len(cuts)))
        level = level * jnp.repeat(steps, dims[axis_at] // blocks).reshape([-1 if axis == axis_at else 1 for axis in range(len(dims))])
    return level


def scatter_about(own_key, shape, deviation, reach, cuts=(), kind=jnp.bfloat16):
    loudness = block_scale(own_key, shape, cuts, -0.22, 0.18) if cuts else 1.0
    entries = jax.random.normal(own_key, shape, jnp.float32) * deviation * loudness
    return jnp.minimum(jnp.maximum(entries, -reach), reach).astype(kind)


def setup_inputs(seed: int = 0) -> dict:
    key_of = jax.random.split(jax.random.key(seed), 8)
    stream = draw_stream(jax.random.fold_in(key_of[7], 71), 0)
    key_gate = scatter_about(key_of[1], (SEQ, D), 1.0, 6.0, ((0, 8), (1, 4)))
    query_gate = scatter_about(key_of[2], (SEQ, D), 1.0, 6.0, ((0, 8), (1, 4)))
    grad_output = draw_grad_output(jax.random.fold_in(key_of[7], 71), 0)
    norm_gain = jnp.clip(1.0 + 0.18 * jax.random.normal(key_of[4], (D,), jnp.float32), 0.1, 1.9)
    residue = draw_residue(jax.random.fold_in(key_of[7], 71), 0)
    log_rate = draw_log_rate(jax.random.fold_in(key_of[7], 71), 0)
    return {"stream": stream, "key_gate": key_gate, "query_gate": query_gate, "grad_output": grad_output, "norm_gain": norm_gain, "residue": residue, "log_rate": log_rate}


epsilon = 1e-05

def filter_group(signal, grad_conv, residue, log_rate):
    length = signal.shape[1]
    decay_rate = jnp.exp(log_rate)
    lags = jnp.arange(length, dtype=jnp.float32)
    powers = jnp.exp(-decay_rate[:, :, None] * lags)
    kernel = jnp.einsum('cm,cmd->cd', residue, powers, precision=lax.Precision.HIGHEST)
    fft_size = 2 * length
    spec_signal = jnp.fft.rfft(signal, fft_size, axis=1)
    spec_kernel = jnp.fft.rfft(kernel, fft_size, axis=1)
    spec_grad = jnp.fft.rfft(grad_conv, fft_size, axis=1)
    conv = jnp.fft.irfft(spec_signal * spec_kernel, fft_size, axis=1)[:, :length]
    grad_signal = jnp.fft.irfft(jnp.conj(spec_kernel) * spec_grad, fft_size, axis=1)[:, :length]
    grad_kernel = jnp.fft.irfft(jnp.conj(spec_signal) * spec_grad, fft_size, axis=1)[:, :length]
    grad_residue = jnp.einsum('cd,cmd->cm', grad_kernel, powers, precision=lax.Precision.HIGHEST)
    weighted = jnp.einsum('cd,cmd->cm', grad_kernel * lags, powers, precision=lax.Precision.HIGHEST)
    grad_rate = -decay_rate * residue * weighted
    return (conv, grad_signal, grad_residue, grad_rate)

def reference(stream, key_gate, query_gate, grad_output, norm_gain, residue, log_rate):
    wide_stream = stream.astype(jnp.float32)
    inv_rms = lax.rsqrt(lax.optimization_barrier(jnp.mean(wide_stream * wide_stream, axis=1, keepdims=True)) + epsilon)
    unit_stream = wide_stream * inv_rms
    normed = unit_stream * norm_gain
    key_wide = key_gate.astype(jnp.float32)
    query_wide = query_gate.astype(jnp.float32)
    grad_wide = grad_output.astype(jnp.float32)
    signal = (key_wide * normed).astype(jnp.bfloat16)
    grad_conv = grad_wide * query_wide
    length, channels = stream.shape
    group_size = min(64, channels)
    groups = channels // group_size

    def per_group(items):
        return filter_group(items[0], items[1], items[2], items[3])
    results = lax.map(per_group, (signal.astype(jnp.float32).T.reshape(groups, group_size, length), grad_conv.T.reshape(groups, group_size, length), residue.reshape(groups, group_size, MODES), log_rate.reshape(groups, group_size, MODES)))
    conv = results[0].reshape(channels, length).T
    grad_signal = results[1].reshape(channels, length).T
    scale = 1.0 / math.sqrt(SEQ)
    grad_residue = results[2].reshape(channels, MODES) * scale
    grad_rate = results[3].reshape(channels, MODES) * scale
    output = (query_wide * conv).astype(jnp.bfloat16)
    grad_query = (grad_wide * conv).astype(jnp.bfloat16)
    grad_key = (grad_signal * normed).astype(jnp.bfloat16)
    grad_normed = grad_signal * key_wide
    grad_gain = lax.optimization_barrier(jnp.sum(grad_normed * unit_stream, axis=0)) * scale
    grad_unit = grad_normed * norm_gain
    inner = lax.optimization_barrier(jnp.sum(grad_unit * unit_stream, axis=1, keepdims=True)) / D
    grad_stream = (inv_rms * (grad_unit - unit_stream * inner)).astype(jnp.bfloat16)
    return (output, grad_stream, grad_key, grad_query, grad_gain, grad_residue, grad_rate)
```

```python
import functools
import math

import jax
import jax.numpy as jnp
from jax import lax
from jax.experimental import pallas as pl
from jax.experimental.pallas import tpu as pltpu
from jax.sharding import PartitionSpec as P

D = 4096
MODES = 16
epsilon = 1e-05
LANES = 128
RB = 16
UNROLL = 8
GROUP = 8
MESH = pl.DeviceIdType.MESH
F32 = jnp.float32


def kernel(
    n, nch, rows, kt,
    stream, key, query, gout, gain, res, lrate,
    out, gstream, gkey, gquery, ggain, gres, grate,
    xs, gs, ys, ss, qbuf, apow, alen, col, inv_col, in_row, nrm_buf, inner_buf,
    sbuf, tbuf, state, part, rsbuf, agbuf, gainbuf,
    nrm_s, nrm_r, inner_s, inner_r, s_s, s_r, t_s, t_r, rs_s, rs_r, ag_s, ag_r, gn_s, gn_r,
):
    me = lax.axis_index("ctx")
    mc = lax.axis_index("ch")
    nblk = rows // RB
    nstep = rows // UNROLL
    per = 2 * MODES // n

    def each(count, test, fn):
        def body(j, carry):
            @pl.when(test(j))
            def _():
                fn(j)

            return carry

        lax.fori_loop(0, count, body, 0)

    def remote(src, dst, ssem, rsem, axis, j):
        return pltpu.make_async_remote_copy(
            src_ref=src, dst_ref=dst, send_sem=ssem, recv_sem=rsem,
            device_id={axis: j}, device_id_type=MESH,
        )

    def c_nrm(j):
        return remote(nrm_buf.at[mc], nrm_buf.at[mc], nrm_s.at[j], nrm_r.at[mc], "ch", j)

    def w_nrm(j):
        return remote(nrm_buf.at[j], nrm_buf.at[j], nrm_s.at[j], nrm_r.at[j], "ch", j)

    def c_inner(j):
        return remote(inner_buf.at[mc], inner_buf.at[mc], inner_s.at[j], inner_r.at[mc], "ch", j)

    def w_inner(j):
        return remote(inner_buf.at[j], inner_buf.at[j], inner_s.at[j], inner_r.at[j], "ch", j)

    def c_s(j):
        return remote(sbuf.at[me], sbuf.at[me], s_s.at[j], s_r.at[me], "ctx", j)

    def w_s(j):
        return remote(sbuf.at[j], sbuf.at[j], s_s.at[j], s_r.at[j], "ctx", j)

    def c_t(j):
        return remote(tbuf.at[me], tbuf.at[me], t_s.at[j], t_r.at[me], "ctx", j)

    def w_t(j):
        return remote(tbuf.at[j], tbuf.at[j], t_s.at[j], t_r.at[j], "ctx", j)

    def c_rs(j):
        return remote(part.at[pl.ds(j * per, per)], rsbuf.at[me], rs_s.at[j], rs_r.at[me], "ctx", j)

    def w_rs(j):
        return remote(rsbuf.at[j], rsbuf.at[j], rs_s.at[j], rs_r.at[j], "ctx", j)

    def c_ag(j):
        return remote(agbuf.at[me], agbuf.at[me], ag_s.at[j], ag_r.at[me], "ctx", j)

    def w_ag(j):
        return remote(agbuf.at[j], agbuf.at[j], ag_s.at[j], ag_r.at[j], "ctx", j)

    def c_gn(j):
        return remote(gainbuf.at[me], gainbuf.at[me], gn_s.at[j], gn_r.at[me], "ctx", j)

    def w_gn(j):
        return remote(gainbuf.at[j], gainbuf.at[j], gn_s.at[j], gn_r.at[j], "ctx", j)

    barrier = pltpu.get_barrier_semaphore()
    each(n, lambda j: j != me, lambda j: pl.semaphore_signal(
        barrier, inc=1, device_id={"ctx": j}, device_id_type=MESH))
    each(nch, lambda j: j != mc, lambda j: pl.semaphore_signal(
        barrier, inc=1, device_id={"ch": j}, device_id_type=MESH))

    rate = jnp.exp(lrate[...])
    apow[...] = jnp.exp(-rate)
    alen[...] = jnp.exp(-rate * float(rows))

    def lanes(k):
        return pl.ds(k * LANES, LANES)

    def rows_of(b):
        return pl.ds(pl.multiple_of(b * RB, RB), RB)

    def spread(b, k):
        return pl.ds(b * (RB * kt) + k, RB, stride=kt)

    def at(t):
        return pl.ds(pl.multiple_of(t * kt, kt), kt)

    def to_row(ref):
        return jnp.broadcast_to(jnp.sum(ref[...].T, axis=0, keepdims=True), (8, rows))

    def first(b, carry):
        r = rows_of(b)
        total = jnp.zeros((RB, LANES), F32)
        for k in range(kt):
            s = stream[r, lanes(k)].astype(F32)
            total += s * s
            gs[spread(b, k), :] = gout[r, lanes(k)].astype(F32) * query[r, lanes(k)].astype(F32)
        col[r, :] = total
        return carry

    lax.fori_loop(0, nblk, first, 0)
    nrm_buf[mc] = to_row(col)
    pl.semaphore_wait(barrier, n - 1 + nch - 1)
    each(nch, lambda j: j != mc, lambda j: c_nrm(j).start())

    def end_state(src, backward):
        a = [apow[m] for m in range(MODES)]

        def body(i, carry):
            h = list(carry)
            for u in range(UNROLL):
                t = i * UNROLL + u
                x = src[at(rows - 1 - t if backward else t), :]
                for m in range(MODES):
                    h[m] = a[m] * h[m] + x
            return tuple(h)

        zero = jnp.zeros((kt, LANES), F32)
        return lax.fori_loop(0, nstep, body, (zero,) * MODES)

    ends = end_state(gs, True)
    for m in range(MODES):
        tbuf[me, m] = ends[m]
    each(n, lambda j: j < me, lambda j: c_t(j).start())

    each(nch, lambda j: j != mc, lambda j: w_nrm(j).wait_recv())
    total = nrm_buf[0]
    for j in range(1, nch):
        total = total + nrm_buf[j]
    inv_row = lax.rsqrt(total / D + epsilon)
    inv_col[...] = jnp.broadcast_to(inv_row[0:1], (LANES, rows)).T

    def second(b, carry):
        r = rows_of(b)
        iv = inv_col[r, :]
        for k in range(kt):
            normed = stream[r, lanes(k)].astype(F32) * iv * gain[k : k + 1, :]
            x = (key[r, lanes(k)].astype(F32) * normed).astype(jnp.bfloat16)
            xs[spread(b, k), :] = x.astype(F32)
        return carry

    lax.fori_loop(0, nblk, second, 0)
    ends = end_state(xs, False)
    for m in range(MODES):
        sbuf[me, m] = ends[m]
    each(n, lambda j: j > me, lambda j: c_s(j).start())

    def backward(group):
        m0 = group * GROUP
        a = [apow[m0 + m] for m in range(GROUP)]
        c = [res[m0 + m] for m in range(GROUP)]

        def body(i, carry):
            q = list(carry)
            for u in range(UNROLL):
                t = rows - 1 - (i * UNROLL + u)
                g = gs[at(t), :]
                acc = ss[at(t), :] if group else None
                for m in range(GROUP):
                    q[m] = a[m] * q[m] + g
                    qbuf[t, m] = q[m]
                    term = c[m] * q[m]
                    acc = term if acc is None else acc + term
                ss[at(t), :] = acc
            return tuple(q)

        lax.fori_loop(0, nstep, body, tuple(state[1, m0 + m] for m in range(GROUP)))

    def forward(group):
        m0 = group * GROUP
        a = [apow[m0 + m] for m in range(GROUP)]
        c = [res[m0 + m] for m in range(GROUP)]
        zero = jnp.zeros((kt, LANES), F32)

        def body(i, carry):
            h, gr, gw = (list(v) for v in carry)
            for u in range(UNROLL):
                t = i * UNROLL + u
                x = xs[at(t), :]
                g = gs[at(t), :]
                acc = ys[at(t), :] if group else None
                for m in range(GROUP):
                    z = a[m] * h[m]
                    gw[m] = gw[m] + z * qbuf[t, m]
                    h[m] = z + x
                    gr[m] = gr[m] + g * h[m]
                    term = c[m] * h[m]
                    acc = term if acc is None else acc + term
                ys[at(t), :] = acc
            return tuple(h), tuple(gr), tuple(gw)

        start = tuple(state[0, m0 + m] for m in range(GROUP))
        unused, gr, gw = lax.fori_loop(0, nstep, body, (start, (zero,) * GROUP, (zero,) * GROUP))
        for m in range(GROUP):
            part[m0 + m] = gr[m]
            part[MODES + m0 + m] = gw[m]

    state[...] = jnp.zeros_like(state)

    def take_t(i):
        j = n - 1 - i
        w_t(j).wait_recv()
        state[1] = alen[...] * state[1] + tbuf[j]

    each(n, lambda i: n - 1 - i > me, take_t)
    backward(0)

    def take_s(j):
        w_s(j).wait_recv()
        state[0] = alen[...] * state[0] + sbuf[j]

    each(n, lambda j: j < me, take_s)
    forward(0)
    for group in range(1, MODES // GROUP - 1):
        backward(group)
        forward(group)
    backward(MODES // GROUP - 1)

    def third(b, carry):
        r = rows_of(b)
        iv = inv_col[r, :]
        total = jnp.zeros((RB, LANES), F32)
        gains = list(carry)
        for k in range(kt):
            unit = stream[r, lanes(k)].astype(F32) * iv
            gk = gain[k : k + 1, :]
            sig = ss[spread(b, k), :]
            gkey[r, lanes(k)] = (sig * (unit * gk)).astype(jnp.bfloat16)
            prod = sig * key[r, lanes(k)].astype(F32) * unit
            gains[k] = gains[k] + prod
            total += prod * gk
        col[r, :] = total
        return tuple(gains)

    gains = lax.fori_loop(0, nblk, third, (jnp.zeros((RB, LANES), F32),) * kt)
    for k in range(kt):
        gainbuf[me, k : k + 1, :] = jnp.sum(gains[k], axis=0, keepdims=True)
    inner_buf[mc] = to_row(col)
    each(nch, lambda j: j != mc, lambda j: c_inner(j).start())
    each(n, lambda j: j != me, lambda j: c_gn(j).start())

    forward(MODES // GROUP - 1)
    rsbuf[me] = part[pl.ds(me * per, per)]
    each(n, lambda j: j != me, lambda j: c_rs(j).start())

    def fourth(b, carry):
        r = rows_of(b)
        for k in range(kt):
            conv = ys[spread(b, k), :]
            out[r, lanes(k)] = (query[r, lanes(k)].astype(F32) * conv).astype(jnp.bfloat16)
            gquery[r, lanes(k)] = (gout[r, lanes(k)].astype(F32) * conv).astype(jnp.bfloat16)
        return carry

    lax.fori_loop(0, nblk, fourth, 0)

    each(n, lambda j: j != me, lambda j: w_rs(j).wait_recv())
    agbuf[me] = lax.fori_loop(
        1, n, lambda j, acc: acc + rsbuf[j], rsbuf[0])
    each(n, lambda j: j != me, lambda j: c_ag(j).start())

    each(nch, lambda j: j != mc, lambda j: w_inner(j).wait_recv())
    total = inner_buf[0]
    for j in range(1, nch):
        total = total + inner_buf[j]
    col[...] = jnp.broadcast_to((total / D)[0:1], (LANES, rows)).T

    def fifth(b, carry):
        r = rows_of(b)
        iv = inv_col[r, :]
        inner = col[r, :]
        for k in range(kt):
            unit = stream[r, lanes(k)].astype(F32) * iv
            unit_grad = ss[spread(b, k), :] * key[r, lanes(k)].astype(F32) * gain[k : k + 1, :]
            gstream[r, lanes(k)] = (iv * (unit_grad - unit * inner)).astype(jnp.bfloat16)
        return carry

    lax.fori_loop(0, nblk, fifth, 0)

    scale = 1.0 / math.sqrt(rows * n)
    each(n, lambda j: j != me, lambda j: w_gn(j).wait_recv())
    ggain[...] = lax.fori_loop(1, n, lambda j, acc: acc + gainbuf[j], gainbuf[0]) * scale
    each(n, lambda j: j != me, lambda j: w_ag(j).wait_recv())
    for m in range(MODES):
        gres[m] = agbuf[m // per, m % per] * scale
        w = MODES + m
        grate[m] = -jnp.exp(lrate[m]) * res[m] * (agbuf[w // per, w % per] * scale)

    each(nch, lambda j: j != mc, lambda j: c_nrm(j).wait_send())
    each(nch, lambda j: j != mc, lambda j: c_inner(j).wait_send())
    each(n, lambda j: j < me, lambda j: c_t(j).wait_send())
    each(n, lambda j: j > me, lambda j: c_s(j).wait_send())
    each(n, lambda j: j != me, lambda j: c_gn(j).wait_send())
    each(n, lambda j: j != me, lambda j: c_rs(j).wait_send())
    each(n, lambda j: j != me, lambda j: c_ag(j).wait_send())


def local(n, nch, stream, key_gate, query_gate, grad_output, norm_gain, residue, log_rate):
    rows, channels = stream.shape
    kt = channels // LANES
    per = 2 * MODES // n
    vm = pl.BlockSpec(memory_space=pltpu.VMEM)
    wide = jax.ShapeDtypeStruct((rows, channels), jnp.bfloat16)
    modal = jax.ShapeDtypeStruct((MODES, kt, LANES), F32)
    dma = pltpu.SemaphoreType.DMA
    flat = pltpu.VMEM((rows * kt, LANES), F32)
    one = pltpu.VMEM((rows, LANES), F32)
    lined = pltpu.VMEM((nch, 8, rows), F32)
    ends = pltpu.VMEM((n, MODES, kt, LANES), F32)
    mode = pltpu.VMEM((MODES, kt, LANES), F32)
    pieces = pltpu.VMEM((n, per, kt, LANES), F32)
    out, gstream, gkey, gquery, ggain, gres, grate = pl.pallas_call(
        functools.partial(kernel, n, nch, rows, kt),
        out_shape=(wide, wide, wide, wide, jax.ShapeDtypeStruct((kt, LANES), F32), modal, modal),
        in_specs=[vm] * 7,
        out_specs=(vm,) * 7,
        scratch_shapes=[
            flat, flat, flat, flat,
            pltpu.VMEM((rows, GROUP, kt, LANES), F32),
            mode, mode, one, one,
            pltpu.VMEM((8, rows), F32),
            lined, lined, ends, ends,
            pltpu.VMEM((2, MODES, kt, LANES), F32),
            pltpu.VMEM((2 * MODES, kt, LANES), F32),
            pieces, pieces,
            pltpu.VMEM((n, kt, LANES), F32),
            dma((nch,)), dma((nch,)), dma((nch,)), dma((nch,)),
        ] + [dma((n,))] * 10,
        compiler_params=pltpu.CompilerParams(
            collective_id=0, has_side_effects=True, vmem_limit_bytes=56 * 2**20
        ),
    )(
        stream, key_gate, query_gate, grad_output,
        norm_gain.reshape(kt, LANES),
        residue.T.reshape(MODES, kt, LANES),
        log_rate.T.reshape(MODES, kt, LANES),
    )
    return (
        out, gstream, gkey, gquery, ggain.reshape(channels),
        gres.reshape(MODES, channels).T, grate.reshape(MODES, channels).T,
    )


def solution(mesh):
    wide = P("ctx", "ch")
    thin = P("ch", None)
    return jax.shard_map(
        functools.partial(local, mesh.shape["ctx"], mesh.shape["ch"]),
        mesh=mesh,
        in_specs=(wide, wide, wide, wide, P("ch"), thin, thin),
        out_specs=(wide, wide, wide, wide, P("ch"), thin, thin),
        check_vma=False,
    )
```

```python
import functools
import math

import jax
import jax.numpy as jnp
from jax import lax
from jax.experimental import pallas as pl
from jax.experimental.pallas import tpu as pltpu
from jax.sharding import PartitionSpec as P

D = 4096
MODES = 16
epsilon = 1e-05
LANES = 128
RB = 16
UNROLL = 8
GROUP = 8
MESH = pl.DeviceIdType.MESH
F32 = jnp.float32


def kernel(
    n, nch, rows, kt,
    stream_in, key_in, query_in, gout_in, gain, res_in, lrate_in,
    conv_out, sig_out, inv_out, inner_out, ggain, gmode,
    stream, key, query, gout, xs, gs, ys, ss, qbuf, res, lrate, apow, alen,
    col, inv_col, nrm_buf, inner_buf, io_s,
    sbuf, tbuf, state, part, rsbuf, agbuf, gainbuf,
    nrm_s, nrm_r, inner_s, inner_r, s_s, s_r, t_s, t_r, rs_s, rs_r, ag_s, ag_r, gn_s, gn_r,
):
    me = lax.axis_index("ctx")
    mc = lax.axis_index("ch")
    nblk = rows // RB
    nstep = rows // UNROLL
    per = 2 * MODES // n

    def each(count, test, fn):
        def body(j, carry):
            @pl.when(test(j))
            def _():
                fn(j)

            return carry

        lax.fori_loop(0, count, body, 0)

    def remote(src, dst, ssem, rsem, axis, j):
        return pltpu.make_async_remote_copy(
            src_ref=src, dst_ref=dst, send_sem=ssem, recv_sem=rsem,
            device_id={axis: j}, device_id_type=MESH,
        )

    def c_nrm(j):
        return remote(nrm_buf.at[mc], nrm_buf.at[mc], nrm_s.at[j], nrm_r.at[mc], "ch", j)

    def w_nrm(j):
        return remote(nrm_buf.at[j], nrm_buf.at[j], nrm_s.at[j], nrm_r.at[j], "ch", j)

    def c_inner(j):
        return remote(inner_buf.at[mc], inner_buf.at[mc], inner_s.at[j], inner_r.at[mc], "ch", j)

    def w_inner(j):
        return remote(inner_buf.at[j], inner_buf.at[j], inner_s.at[j], inner_r.at[j], "ch", j)

    def c_s(j):
        return remote(sbuf.at[me], sbuf.at[me], s_s.at[j], s_r.at[me], "ctx", j)

    def w_s(j):
        return remote(sbuf.at[j], sbuf.at[j], s_s.at[j], s_r.at[j], "ctx", j)

    def c_t(j):
        return remote(tbuf.at[me], tbuf.at[me], t_s.at[j], t_r.at[me], "ctx", j)

    def w_t(j):
        return remote(tbuf.at[j], tbuf.at[j], t_s.at[j], t_r.at[j], "ctx", j)

    def c_rs(j):
        return remote(part.at[pl.ds(j * per, per)], rsbuf.at[me], rs_s.at[j], rs_r.at[me], "ctx", j)

    def w_rs(j):
        return remote(rsbuf.at[j], rsbuf.at[j], rs_s.at[j], rs_r.at[j], "ctx", j)

    def c_ag(j):
        return remote(agbuf.at[me], agbuf.at[me], ag_s.at[j], ag_r.at[me], "ctx", j)

    def w_ag(j):
        return remote(agbuf.at[j], agbuf.at[j], ag_s.at[j], ag_r.at[j], "ctx", j)

    def c_gn(j):
        return remote(gainbuf.at[me], gainbuf.at[me], gn_s.at[j], gn_r.at[me], "ctx", j)

    def w_gn(j):
        return remote(gainbuf.at[j], gainbuf.at[j], gn_s.at[j], gn_r.at[j], "ctx", j)

    reads = [
        pltpu.make_async_copy(src, dst, io_s.at[i])
        for i, (src, dst) in enumerate(
            ((stream_in, stream), (gout_in, gout), (query_in, query), (key_in, key))
        )
    ]
    for copy in reads:
        copy.start()
    writes = [
        pltpu.make_async_copy(src, dst, io_s.at[4 + i])
        for i, (src, dst) in enumerate(((inv_col, inv_out), (ss, sig_out), (ys, conv_out), (col, inner_out)))
    ]

    barrier = pltpu.get_barrier_semaphore()
    each(n, lambda j: j != me, lambda j: pl.semaphore_signal(
        barrier, inc=1, device_id={"ctx": j}, device_id_type=MESH))
    each(nch, lambda j: j != mc, lambda j: pl.semaphore_signal(
        barrier, inc=1, device_id={"ch": j}, device_id_type=MESH))

    for k in range(kt):
        mode_rows = pl.ds(k, MODES, stride=kt)
        res[mode_rows, :] = res_in[:, k * LANES : (k + 1) * LANES]
        lrate[mode_rows, :] = lrate_in[:, k * LANES : (k + 1) * LANES]
    rate = jnp.exp(lrate[...])
    apow[...] = jnp.exp(-rate)
    alen[...] = jnp.exp(-rate * float(rows))

    def lanes(k):
        return pl.ds(k * LANES, LANES)

    def rows_of(b):
        return pl.ds(pl.multiple_of(b * RB, RB), RB)

    def spread(b, k):
        return pl.ds(b * (RB * kt) + k, RB, stride=kt)

    def at(t):
        return pl.ds(pl.multiple_of(t * kt, kt), kt)

    def to_row(ref):
        return jnp.broadcast_to(jnp.sum(ref[...].T, axis=0, keepdims=True), (8, rows))

    def first(b, carry):
        r = rows_of(b)
        total = jnp.zeros((RB, LANES), F32)
        for k in range(kt):
            s = stream[r, lanes(k)].astype(F32)
            total += s * s
        col[r, :] = total
        return carry

    reads[0].wait()
    lax.fori_loop(0, nblk, first, 0)
    nrm_buf[mc] = to_row(col)
    pl.semaphore_wait(barrier, n - 1 + nch - 1)
    each(nch, lambda j: j != mc, lambda j: c_nrm(j).start())

    def cotangent(b, carry):
        r = rows_of(b)
        for k in range(kt):
            gs[spread(b, k), :] = gout[r, lanes(k)].astype(F32) * query[r, lanes(k)].astype(F32)
        return carry

    reads[1].wait()
    reads[2].wait()
    lax.fori_loop(0, nblk, cotangent, 0)

    def mode(ref, m):
        return ref[m * kt : (m + 1) * kt, :]

    def tree(terms):
        while len(terms) > 1:
            terms = [sum(terms[i + 1 : i + 2], terms[i]) for i in range(0, len(terms), 2)]
        return terms[0]

    def end_state(src, backward):
        a = [mode(apow, m) for m in range(MODES)]

        def body(i, carry):
            h = list(carry)
            for u in range(UNROLL):
                t = i * UNROLL + u
                x = src[at(rows - 1 - t if backward else t), :]
                for m in range(MODES):
                    h[m] = a[m] * h[m] + x
            return tuple(h)

        zero = jnp.zeros((kt, LANES), F32)
        return lax.fori_loop(0, nstep, body, (zero,) * MODES)

    ends = end_state(gs, True)
    for m in range(MODES):
        tbuf[me, m * kt : (m + 1) * kt, :] = ends[m]
    each(n, lambda j: j < me, lambda j: c_t(j).start())

    each(nch, lambda j: j != mc, lambda j: w_nrm(j).wait_recv())
    total = nrm_buf[0]
    for j in range(1, nch):
        total = total + nrm_buf[j]
    inv_row = lax.rsqrt(total / D + epsilon)
    inv_col[...] = jnp.broadcast_to(inv_row[0:1], (LANES, rows)).T
    writes[0].start()
    reads[3].wait()

    def second(b, carry):
        r = rows_of(b)
        iv = inv_col[r, :]
        for k in range(kt):
            normed = stream[r, lanes(k)].astype(F32) * iv * gain[k : k + 1, :]
            x = (key[r, lanes(k)].astype(F32) * normed).astype(jnp.bfloat16)
            xs[spread(b, k), :] = x.astype(F32)
        return carry

    lax.fori_loop(0, nblk, second, 0)
    ends = end_state(xs, False)
    for m in range(MODES):
        sbuf[me, m * kt : (m + 1) * kt, :] = ends[m]
    each(n, lambda j: j > me, lambda j: c_s(j).start())

    def backward(group):
        m0 = group * GROUP
        a = [mode(apow, m0 + m) for m in range(GROUP)]
        c = [mode(res, m0 + m) for m in range(GROUP)]

        def body(i, carry):
            q = list(carry)
            for u in range(UNROLL):
                t = rows - 1 - (i * UNROLL + u)
                g = gs[at(t), :]
                terms = [ss[at(t), :]] if group else []
                for m in range(GROUP):
                    q[m] = a[m] * q[m] + g
                    qbuf[t, m0 + m] = q[m]
                    terms.append(c[m] * q[m])
                ss[at(t), :] = tree(terms)
            return tuple(q)

        lax.fori_loop(0, nstep, body, tuple(mode(state.at[1], m0 + m) for m in range(GROUP)))

    def forward(group):
        m0 = group * GROUP
        a = [mode(apow, m0 + m) for m in range(GROUP)]
        c = [mode(res, m0 + m) for m in range(GROUP)]
        zero = jnp.zeros((kt, LANES), F32)

        def body(i, carry):
            h, gr, gw = (list(v) for v in carry)
            for u in range(UNROLL):
                t = i * UNROLL + u
                x = xs[at(t), :]
                g = gs[at(t), :]
                terms = [ys[at(t), :]] if group else []
                for m in range(GROUP):
                    z = a[m] * h[m]
                    gw[m] = gw[m] + z * qbuf[t, m0 + m]
                    h[m] = z + x
                    gr[m] = gr[m] + g * h[m]
                    terms.append(c[m] * h[m])
                ys[at(t), :] = tree(terms)
            return tuple(h), tuple(gr), tuple(gw)

        start = tuple(mode(state.at[0], m0 + m) for m in range(GROUP))
        unused, gr, gw = lax.fori_loop(0, nstep, body, (start, (zero,) * GROUP, (zero,) * GROUP))
        for m in range(GROUP):
            part[m0 + m] = gr[m]
            part[MODES + m0 + m] = gw[m]

    state[...] = jnp.zeros_like(state)

    def take_t(i):
        j = n - 1 - i
        w_t(j).wait_recv()
        state[1] = alen[...] * state[1] + tbuf[j]

    each(n, lambda i: n - 1 - i > me, take_t)
    for group in range(MODES // GROUP):
        backward(group)
    writes[1].start()

    def take_s(j):
        w_s(j).wait_recv()
        state[0] = alen[...] * state[0] + sbuf[j]

    each(n, lambda j: j < me, take_s)
    for group in range(MODES // GROUP):
        forward(group)
    writes[2].start()
    rsbuf[me] = part[pl.ds(me * per, per)]
    each(n, lambda j: j != me, lambda j: c_rs(j).start())

    def third(b, carry):
        r = rows_of(b)
        iv = inv_col[r, :]
        total = jnp.zeros((RB, LANES), F32)
        gains = list(carry)
        for k in range(kt):
            unit = stream[r, lanes(k)].astype(F32) * iv
            prod = ss[spread(b, k), :] * key[r, lanes(k)].astype(F32) * unit
            gains[k] = gains[k] + prod
            total += prod * gain[k : k + 1, :]
        col[r, :] = total
        return tuple(gains)

    gains = lax.fori_loop(0, nblk, third, (jnp.zeros((RB, LANES), F32),) * kt)
    inner_buf[mc] = to_row(col)
    each(nch, lambda j: j != mc, lambda j: c_inner(j).start())
    for k in range(kt):
        gainbuf[me, k : k + 1, :] = jnp.sum(gains[k], axis=0, keepdims=True)
    each(n, lambda j: j != me, lambda j: c_gn(j).start())

    each(n, lambda j: j != me, lambda j: w_rs(j).wait_recv())
    agbuf[me] = lax.fori_loop(1, n, lambda j, acc: acc + rsbuf[j], rsbuf[0])
    each(n, lambda j: j != me, lambda j: c_ag(j).start())

    each(nch, lambda j: j != mc, lambda j: w_inner(j).wait_recv())
    total = inner_buf[0]
    for j in range(1, nch):
        total = total + inner_buf[j]
    col[...] = jnp.broadcast_to((total / D)[0:1], (LANES, rows)).T
    writes[3].start()

    scale = 1.0 / math.sqrt(rows * n)
    each(n, lambda j: j != me, lambda j: w_gn(j).wait_recv())
    ggain[...] = lax.fori_loop(1, n, lambda j, acc: acc + gainbuf[j], gainbuf[0]) * scale
    each(n, lambda j: j != me, lambda j: w_ag(j).wait_recv())
    for m in range(2 * MODES):
        gmode[m * kt : (m + 1) * kt, :] = agbuf[m // per, m % per] * scale

    each(nch, lambda j: j != mc, lambda j: c_nrm(j).wait_send())
    each(nch, lambda j: j != mc, lambda j: c_inner(j).wait_send())
    each(n, lambda j: j < me, lambda j: c_t(j).wait_send())
    each(n, lambda j: j > me, lambda j: c_s(j).wait_send())
    each(n, lambda j: j != me, lambda j: c_gn(j).wait_send())
    each(n, lambda j: j != me, lambda j: c_rs(j).wait_send())
    each(n, lambda j: j != me, lambda j: c_ag(j).wait_send())
    for copy in writes:
        copy.wait()


def finish(
    kt,
    stream, key, query, gout, conv, sig, inv, inner, gain, res, lrate, ggain_in, gmode,
    out, gstream, gkey, gquery, ggain, gres, grate,
):
    @pl.when(pl.program_id(0) == 0)
    def _():
        ggain[...] = ggain_in[...]
        for k in range(kt):
            cols = slice(k * LANES, (k + 1) * LANES)
            gres[:, cols] = gmode[pl.ds(k, MODES, stride=kt), :]
            weighted = gmode[pl.ds(MODES * kt + k, MODES, stride=kt), :]
            grate[:, cols] = -jnp.exp(lrate[:, cols]) * res[:, cols] * weighted

    def body(b, carry):
        r = pl.ds(pl.multiple_of(b * RB, RB), RB)
        iv = inv[r, :]
        mean = inner[r, :]
        for k in range(kt):
            cols = pl.ds(k * LANES, LANES)
            spread = pl.ds(b * (RB * kt) + k, RB, stride=kt)
            gk = gain[k : k + 1, :]
            conv_k = conv[spread, :]
            sig_k = sig[spread, :]
            unit = stream[r, cols].astype(F32) * iv
            out[r, cols] = (query[r, cols].astype(F32) * conv_k).astype(jnp.bfloat16)
            gquery[r, cols] = (gout[r, cols].astype(F32) * conv_k).astype(jnp.bfloat16)
            gkey[r, cols] = (sig_k * (unit * gk)).astype(jnp.bfloat16)
            unit_grad = sig_k * key[r, cols].astype(F32) * gk
            gstream[r, cols] = (iv * (unit_grad - unit * mean)).astype(jnp.bfloat16)
        return carry

    lax.fori_loop(0, stream.shape[0] // RB, body, 0)


def local(n, nch, stream, key_gate, query_gate, grad_output, norm_gain, residue, log_rate):
    rows, channels = stream.shape
    kt = channels // LANES
    per = 2 * MODES // n
    vm = pl.BlockSpec(memory_space=pltpu.VMEM)
    anywhere = pl.BlockSpec(memory_space=pl.ANY)
    wide = jax.ShapeDtypeStruct((rows, channels), jnp.bfloat16)
    flat_out = jax.ShapeDtypeStruct((rows * kt, LANES), F32)
    one_out = jax.ShapeDtypeStruct((rows, LANES), F32)
    gain_out = jax.ShapeDtypeStruct((kt, LANES), F32)
    mode_out = jax.ShapeDtypeStruct((2 * MODES * kt, LANES), F32)
    dma = pltpu.SemaphoreType.DMA
    held = pltpu.VMEM((rows, channels), jnp.bfloat16)
    flat = pltpu.VMEM((rows * kt, LANES), F32)
    one = pltpu.VMEM((rows, LANES), F32)
    lined = pltpu.VMEM((nch, 8, rows), F32)
    ends = pltpu.VMEM((n, MODES * kt, LANES), F32)
    modal = pltpu.VMEM((MODES * kt, LANES), F32)
    pieces = pltpu.VMEM((n, per, kt, LANES), F32)
    gain = norm_gain.reshape(kt, LANES)
    res, lrate = residue.T, log_rate.T
    conv, sig, inv, inner, ggain, gmode = pl.pallas_call(
        functools.partial(kernel, n, nch, rows, kt),
        out_shape=(flat_out, flat_out, one_out, one_out, gain_out, mode_out),
        in_specs=[anywhere] * 4 + [vm] * 3,
        out_specs=(anywhere,) * 4 + (vm,) * 2,
        scratch_shapes=[
            held, held, held, held,
            flat, flat, flat, flat,
            pltpu.VMEM((rows, MODES, kt, LANES), F32),
            modal, modal, modal, modal, one, one,
            lined, lined, dma((8,)), ends, ends,
            pltpu.VMEM((2, MODES * kt, LANES), F32),
            pltpu.VMEM((2 * MODES, kt, LANES), F32),
            pieces, pieces,
            pltpu.VMEM((n, kt, LANES), F32),
            dma((nch,)), dma((nch,)), dma((nch,)), dma((nch,)),
        ] + [dma((n,))] * 10,
        compiler_params=pltpu.CompilerParams(
            collective_id=0, has_side_effects=True, vmem_limit_bytes=56 * 2**20
        ),
    )(stream, key_gate, query_gate, grad_output, gain, res, lrate)

    step = min(rows, 64)
    wide_spec = pl.BlockSpec((step, channels), lambda i: (i, 0))
    flat_spec = pl.BlockSpec((step * kt, LANES), lambda i: (i, 0))
    one_spec = pl.BlockSpec((step, LANES), lambda i: (i, 0))
    whole = lambda *shape: pl.BlockSpec(shape, lambda i: (0, 0))
    mode_spec = whole(MODES, channels)
    gain_spec = whole(kt, LANES)
    mode_t = jax.ShapeDtypeStruct((MODES, channels), F32)
    out, gstream, gkey, gquery, ggain, gres, grate = pl.pallas_call(
        functools.partial(finish, kt),
        grid=(rows // step,),
        out_shape=(wide, wide, wide, wide, gain_out, mode_t, mode_t),
        in_specs=[wide_spec] * 4 + [flat_spec] * 2 + [one_spec] * 2
        + [gain_spec, mode_spec, mode_spec, gain_spec, whole(2 * MODES * kt, LANES)],
        out_specs=(wide_spec,) * 4 + (gain_spec, mode_spec, mode_spec),
        compiler_params=pltpu.CompilerParams(vmem_limit_bytes=56 * 2**20),
    )(stream, key_gate, query_gate, grad_output, conv, sig, inv, inner, gain, res, lrate, ggain, gmode)
    return out, gstream, gkey, gquery, ggain.reshape(channels), gres.T, grate.T


def solution(mesh):
    wide = P("ctx", "ch")
    thin = P("ch", None)
    return jax.shard_map(
        functools.partial(local, mesh.shape["ctx"], mesh.shape["ch"]),
        mesh=mesh,
        in_specs=(wide, wide, wide, wide, P("ch"), thin, thin),
        out_specs=(wide, wide, wide, wide, P("ch"), thin, thin),
        check_vma=False,
    )
```

```python
import functools
import math

import jax
import jax.numpy as jnp
from jax import lax
from jax.experimental import pallas as pl
from jax.experimental.pallas import tpu as pltpu
from jax.sharding import PartitionSpec as P

D = 4096
MODES = 16
epsilon = 1e-05
LANES = 128
RB = 16
UNROLL = 8
GROUP = 8
PAD = 1
MESH = pl.DeviceIdType.MESH
F32 = jnp.float32


def kernel(
    n, nch, rows, kt,
    stream_in, key_in, query_in, gout_in, gain, res_in, lrate_in,
    conv_out, sig_out, inv_out, inner_out, ggain, gmode,
    stream, key, query, gout, xs, gs, ys, ss, qbuf, res, lrate, apow, alen,
    col, inv_col, nrm_buf, inner_buf, io_s,
    sbuf, tbuf, state, part, rsbuf, agbuf, gainbuf,
    nrm_s, nrm_r, inner_s, inner_r, s_s, s_r, t_s, t_r, rs_s, rs_r, ag_s, ag_r, gn_s, gn_r,
):
    me = lax.axis_index("ctx")
    mc = lax.axis_index("ch")
    nblk = rows // RB
    nstep = rows // UNROLL
    per = 2 * MODES // n
    ps = kt + PAD

    def each(count, test, fn):
        def body(j, carry):
            @pl.when(test(j))
            def _():
                fn(j)

            return carry

        lax.fori_loop(0, count, body, 0)

    def remote(src, dst, ssem, rsem, axis, j):
        return pltpu.make_async_remote_copy(
            src_ref=src, dst_ref=dst, send_sem=ssem, recv_sem=rsem,
            device_id={axis: j}, device_id_type=MESH,
        )

    def c_nrm(j):
        return remote(nrm_buf.at[mc], nrm_buf.at[mc], nrm_s.at[j], nrm_r.at[mc], "ch", j)

    def w_nrm(j):
        return remote(nrm_buf.at[j], nrm_buf.at[j], nrm_s.at[j], nrm_r.at[j], "ch", j)

    def c_inner(j):
        return remote(inner_buf.at[mc], inner_buf.at[mc], inner_s.at[j], inner_r.at[mc], "ch", j)

    def w_inner(j):
        return remote(inner_buf.at[j], inner_buf.at[j], inner_s.at[j], inner_r.at[j], "ch", j)

    def c_s(j):
        return remote(sbuf.at[me], sbuf.at[me], s_s.at[j], s_r.at[me], "ctx", j)

    def w_s(j):
        return remote(sbuf.at[j], sbuf.at[j], s_s.at[j], s_r.at[j], "ctx", j)

    def c_t(j):
        return remote(tbuf.at[me], tbuf.at[me], t_s.at[j], t_r.at[me], "ctx", j)

    def w_t(j):
        return remote(tbuf.at[j], tbuf.at[j], t_s.at[j], t_r.at[j], "ctx", j)

    def c_rs(j):
        return remote(part.at[pl.ds(j * per, per)], rsbuf.at[me], rs_s.at[j], rs_r.at[me], "ctx", j)

    def w_rs(j):
        return remote(rsbuf.at[j], rsbuf.at[j], rs_s.at[j], rs_r.at[j], "ctx", j)

    def c_ag(j):
        return remote(agbuf.at[me], agbuf.at[me], ag_s.at[j], ag_r.at[me], "ctx", j)

    def w_ag(j):
        return remote(agbuf.at[j], agbuf.at[j], ag_s.at[j], ag_r.at[j], "ctx", j)

    def c_gn(j):
        return remote(gainbuf.at[me], gainbuf.at[me], gn_s.at[j], gn_r.at[me], "ctx", j)

    def w_gn(j):
        return remote(gainbuf.at[j], gainbuf.at[j], gn_s.at[j], gn_r.at[j], "ctx", j)

    reads = [
        pltpu.make_async_copy(src, dst, io_s.at[i])
        for i, (src, dst) in enumerate(
            ((stream_in, stream), (gout_in, gout), (query_in, query), (key_in, key))
        )
    ]
    for copy in reads:
        copy.start()
    writes = [
        pltpu.make_async_copy(src, dst, io_s.at[4 + i])
        for i, (src, dst) in enumerate(((inv_col, inv_out), (ss, sig_out), (ys, conv_out), (col, inner_out)))
    ]

    barrier = pltpu.get_barrier_semaphore()
    each(n, lambda j: j != me, lambda j: pl.semaphore_signal(
        barrier, inc=1, device_id={"ctx": j}, device_id_type=MESH))
    each(nch, lambda j: j != mc, lambda j: pl.semaphore_signal(
        barrier, inc=1, device_id={"ch": j}, device_id_type=MESH))

    for k in range(kt):
        mode_rows = pl.ds(k, MODES, stride=kt)
        res[mode_rows, :] = res_in[:, k * LANES : (k + 1) * LANES]
        lrate[mode_rows, :] = lrate_in[:, k * LANES : (k + 1) * LANES]
    rate = jnp.exp(lrate[...])
    apow[...] = jnp.exp(-rate)
    alen[...] = jnp.exp(-rate * float(rows))

    def lanes(k):
        return pl.ds(k * LANES, LANES)

    def rows_of(b):
        return pl.ds(pl.multiple_of(b * RB, RB), RB)

    def spread(b, k):
        return pl.ds(b * (RB * ps) + k, RB, stride=ps)

    def at(t):
        return pl.ds(t * ps, kt)

    def to_row(ref):
        return jnp.broadcast_to(jnp.sum(ref[...].T, axis=0, keepdims=True), (8, rows))

    def first(b, carry):
        r = rows_of(b)
        total = jnp.zeros((RB, LANES), F32)
        for k in range(kt):
            s = stream[r, lanes(k)].astype(F32)
            total += s * s
        col[r, :] = total
        return carry

    reads[0].wait()
    lax.fori_loop(0, nblk, first, 0)
    nrm_buf[mc] = to_row(col)
    pl.semaphore_wait(barrier, n - 1 + nch - 1)
    each(nch, lambda j: j != mc, lambda j: c_nrm(j).start())

    def cotangent(b, carry):
        r = rows_of(b)
        for k in range(kt):
            gs[spread(b, k), :] = gout[r, lanes(k)].astype(F32) * query[r, lanes(k)].astype(F32)
        return carry

    reads[1].wait()
    reads[2].wait()
    lax.fori_loop(0, nblk, cotangent, 0)

    def mode(ref, m):
        return ref[m * kt : (m + 1) * kt, :]

    def tree(terms):
        while len(terms) > 1:
            terms = [sum(terms[i + 1 : i + 2], terms[i]) for i in range(0, len(terms), 2)]
        return terms[0]

    def end_state(src, backward):
        a = [mode(apow, m) for m in range(MODES)]

        def body(i, carry):
            h = list(carry)
            for u in range(UNROLL):
                t = i * UNROLL + u
                x = src[at(rows - 1 - t if backward else t), :]
                for m in range(MODES):
                    h[m] = a[m] * h[m] + x
            return tuple(h)

        zero = jnp.zeros((kt, LANES), F32)
        return lax.fori_loop(0, nstep, body, (zero,) * MODES)

    ends = end_state(gs, True)
    for m in range(MODES):
        tbuf[me, m * kt : (m + 1) * kt, :] = ends[m]
    each(n, lambda j: j < me, lambda j: c_t(j).start())

    each(nch, lambda j: j != mc, lambda j: w_nrm(j).wait_recv())
    total = nrm_buf[0]
    for j in range(1, nch):
        total = total + nrm_buf[j]
    inv_row = lax.rsqrt(total / D + epsilon)
    inv_col[...] = jnp.broadcast_to(inv_row[0:1], (LANES, rows)).T
    writes[0].start()
    reads[3].wait()

    def second(b, carry):
        r = rows_of(b)
        iv = inv_col[r, :]
        for k in range(kt):
            normed = stream[r, lanes(k)].astype(F32) * iv * gain[k : k + 1, :]
            x = (key[r, lanes(k)].astype(F32) * normed).astype(jnp.bfloat16)
            xs[spread(b, k), :] = x.astype(F32)
        return carry

    lax.fori_loop(0, nblk, second, 0)
    ends = end_state(xs, False)
    for m in range(MODES):
        sbuf[me, m * kt : (m + 1) * kt, :] = ends[m]
    each(n, lambda j: j > me, lambda j: c_s(j).start())

    def backward(group):
        m0 = group * GROUP
        a = [mode(apow, m0 + m) for m in range(GROUP)]
        c = [mode(res, m0 + m) for m in range(GROUP)]

        def body(i, carry):
            q = list(carry)
            for u in range(UNROLL):
                t = rows - 1 - (i * UNROLL + u)
                g = gs[at(t), :]
                terms = [ss[at(t), :]] if group else []
                for m in range(GROUP):
                    q[m] = a[m] * q[m] + g
                    qbuf[t, m0 + m] = q[m]
                    terms.append(c[m] * q[m])
                ss[at(t), :] = tree(terms)
            return tuple(q)

        lax.fori_loop(0, nstep, body, tuple(mode(state.at[1], m0 + m) for m in range(GROUP)))

    def forward(group):
        m0 = group * GROUP
        a = [mode(apow, m0 + m) for m in range(GROUP)]
        c = [mode(res, m0 + m) for m in range(GROUP)]
        zero = jnp.zeros((kt, LANES), F32)

        def body(i, carry):
            h, gr, gw = (list(v) for v in carry)
            for u in range(UNROLL):
                t = i * UNROLL + u
                x = xs[at(t), :]
                g = gs[at(t), :]
                terms = [ys[at(t), :]] if group else []
                for m in range(GROUP):
                    z = a[m] * h[m]
                    gw[m] = gw[m] + z * qbuf[t, m0 + m]
                    h[m] = z + x
                    gr[m] = gr[m] + g * h[m]
                    terms.append(c[m] * h[m])
                ys[at(t), :] = tree(terms)
            return tuple(h), tuple(gr), tuple(gw)

        start = tuple(mode(state.at[0], m0 + m) for m in range(GROUP))
        unused, gr, gw = lax.fori_loop(0, nstep, body, (start, (zero,) * GROUP, (zero,) * GROUP))
        for m in range(GROUP):
            part[m0 + m] = gr[m]
            part[MODES + m0 + m] = gw[m]

    state[...] = jnp.zeros_like(state)

    def take_t(i):
        j = n - 1 - i
        w_t(j).wait_recv()
        state[1] = alen[...] * state[1] + tbuf[j]

    each(n, lambda i: n - 1 - i > me, take_t)
    for group in range(MODES // GROUP):
        backward(group)
    writes[1].start()

    def take_s(j):
        w_s(j).wait_recv()
        state[0] = alen[...] * state[0] + sbuf[j]

    each(n, lambda j: j < me, take_s)
    for group in range(MODES // GROUP):
        forward(group)
    writes[2].start()
    rsbuf[me] = part[pl.ds(me * per, per)]
    each(n, lambda j: j != me, lambda j: c_rs(j).start())

    def third(b, carry):
        r = rows_of(b)
        iv = inv_col[r, :]
        total = jnp.zeros((RB, LANES), F32)
        gains = list(carry)
        for k in range(kt):
            unit = stream[r, lanes(k)].astype(F32) * iv
            prod = ss[spread(b, k), :] * key[r, lanes(k)].astype(F32) * unit
            gains[k] = gains[k] + prod
            total += prod * gain[k : k + 1, :]
        col[r, :] = total
        return tuple(gains)

    gains = lax.fori_loop(0, nblk, third, (jnp.zeros((RB, LANES), F32),) * kt)
    inner_buf[mc] = to_row(col)
    each(nch, lambda j: j != mc, lambda j: c_inner(j).start())
    for k in range(kt):
        gainbuf[me, k : k + 1, :] = jnp.sum(gains[k], axis=0, keepdims=True)
    each(n, lambda j: j != me, lambda j: c_gn(j).start())

    each(n, lambda j: j != me, lambda j: w_rs(j).wait_recv())
    agbuf[me] = lax.fori_loop(1, n, lambda j, acc: acc + rsbuf[j], rsbuf[0])
    each(n, lambda j: j != me, lambda j: c_ag(j).start())

    each(nch, lambda j: j != mc, lambda j: w_inner(j).wait_recv())
    total = inner_buf[0]
    for j in range(1, nch):
        total = total + inner_buf[j]
    col[...] = jnp.broadcast_to((total / D)[0:1], (LANES, rows)).T
    writes[3].start()

    scale = 1.0 / math.sqrt(rows * n)
    each(n, lambda j: j != me, lambda j: w_gn(j).wait_recv())
    ggain[...] = lax.fori_loop(1, n, lambda j, acc: acc + gainbuf[j], gainbuf[0]) * scale
    each(n, lambda j: j != me, lambda j: w_ag(j).wait_recv())
    for m in range(2 * MODES):
        gmode[m * kt : (m + 1) * kt, :] = agbuf[m // per, m % per] * scale

    each(nch, lambda j: j != mc, lambda j: c_nrm(j).wait_send())
    each(nch, lambda j: j != mc, lambda j: c_inner(j).wait_send())
    each(n, lambda j: j < me, lambda j: c_t(j).wait_send())
    each(n, lambda j: j > me, lambda j: c_s(j).wait_send())
    each(n, lambda j: j != me, lambda j: c_gn(j).wait_send())
    each(n, lambda j: j != me, lambda j: c_rs(j).wait_send())
    each(n, lambda j: j != me, lambda j: c_ag(j).wait_send())
    for copy in writes:
        copy.wait()


def finish(
    kt,
    stream, key, query, gout, conv, sig, inv, inner, gain, res, lrate, ggain_in, gmode,
    out, gstream, gkey, gquery, ggain, gres, grate,
):
    @pl.when(pl.program_id(0) == 0)
    def _():
        ggain[...] = ggain_in[...]
        for k in range(kt):
            cols = slice(k * LANES, (k + 1) * LANES)
            gres[:, cols] = gmode[pl.ds(k, MODES, stride=kt), :]
            weighted = gmode[pl.ds(MODES * kt + k, MODES, stride=kt), :]
            grate[:, cols] = -jnp.exp(lrate[:, cols]) * res[:, cols] * weighted

    ps = kt + PAD

    def body(b, carry):
        r = pl.ds(pl.multiple_of(b * RB, RB), RB)
        iv = inv[r, :]
        mean = inner[r, :]
        for k in range(kt):
            cols = pl.ds(k * LANES, LANES)
            spread = pl.ds(b * (RB * ps) + k, RB, stride=ps)
            gk = gain[k : k + 1, :]
            conv_k = conv[spread, :]
            sig_k = sig[spread, :]
            unit = stream[r, cols].astype(F32) * iv
            out[r, cols] = (query[r, cols].astype(F32) * conv_k).astype(jnp.bfloat16)
            gquery[r, cols] = (gout[r, cols].astype(F32) * conv_k).astype(jnp.bfloat16)
            gkey[r, cols] = (sig_k * (unit * gk)).astype(jnp.bfloat16)
            unit_grad = sig_k * key[r, cols].astype(F32) * gk
            gstream[r, cols] = (iv * (unit_grad - unit * mean)).astype(jnp.bfloat16)
        return carry

    lax.fori_loop(0, stream.shape[0] // RB, body, 0)


def local(n, nch, stream, key_gate, query_gate, grad_output, norm_gain, residue, log_rate):
    rows, channels = stream.shape
    kt = channels // LANES
    per = 2 * MODES // n
    vm = pl.BlockSpec(memory_space=pltpu.VMEM)
    anywhere = pl.BlockSpec(memory_space=pl.ANY)
    wide = jax.ShapeDtypeStruct((rows, channels), jnp.bfloat16)
    flat_out = jax.ShapeDtypeStruct((rows * (kt + PAD), LANES), F32)
    one_out = jax.ShapeDtypeStruct((rows, LANES), F32)
    gain_out = jax.ShapeDtypeStruct((kt, LANES), F32)
    mode_out = jax.ShapeDtypeStruct((2 * MODES * kt, LANES), F32)
    dma = pltpu.SemaphoreType.DMA
    held = pltpu.VMEM((rows, channels), jnp.bfloat16)
    flat = pltpu.VMEM((rows * (kt + PAD), LANES), F32)
    one = pltpu.VMEM((rows, LANES), F32)
    lined = pltpu.VMEM((nch, 8, rows), F32)
    ends = pltpu.VMEM((n, MODES * kt, LANES), F32)
    modal = pltpu.VMEM((MODES * kt, LANES), F32)
    pieces = pltpu.VMEM((n, per, kt, LANES), F32)
    gain = norm_gain.reshape(kt, LANES)
    res, lrate = residue.T, log_rate.T
    conv, sig, inv, inner, ggain, gmode = pl.pallas_call(
        functools.partial(kernel, n, nch, rows, kt),
        out_shape=(flat_out, flat_out, one_out, one_out, gain_out, mode_out),
        in_specs=[anywhere] * 4 + [vm] * 3,
        out_specs=(anywhere,) * 4 + (vm,) * 2,
        scratch_shapes=[
            held, held, held, held,
            flat, flat, flat, flat,
            pltpu.VMEM((rows, MODES, kt, LANES), F32),
            modal, modal, modal, modal, one, one,
            lined, lined, dma((8,)), ends, ends,
            pltpu.VMEM((2, MODES * kt, LANES), F32),
            pltpu.VMEM((2 * MODES, kt, LANES), F32),
            pieces, pieces,
            pltpu.VMEM((n, kt, LANES), F32),
            dma((nch,)), dma((nch,)), dma((nch,)), dma((nch,)),
        ] + [dma((n,))] * 10,
        compiler_params=pltpu.CompilerParams(
            collective_id=0, has_side_effects=True, vmem_limit_bytes=56 * 2**20
        ),
    )(stream, key_gate, query_gate, grad_output, gain, res, lrate)

    step = min(rows, 64)
    wide_spec = pl.BlockSpec((step, channels), lambda i: (i, 0))
    flat_spec = pl.BlockSpec((step * (kt + PAD), LANES), lambda i: (i, 0))
    one_spec = pl.BlockSpec((step, LANES), lambda i: (i, 0))
    whole = lambda *shape: pl.BlockSpec(shape, lambda i: (0, 0))
    mode_spec = whole(MODES, channels)
    gain_spec = whole(kt, LANES)
    mode_t = jax.ShapeDtypeStruct((MODES, channels), F32)
    out, gstream, gkey, gquery, ggain, gres, grate = pl.pallas_call(
        functools.partial(finish, kt),
        grid=(rows // step,),
        out_shape=(wide, wide, wide, wide, gain_out, mode_t, mode_t),
        in_specs=[wide_spec] * 4 + [flat_spec] * 2 + [one_spec] * 2
        + [gain_spec, mode_spec, mode_spec, gain_spec, whole(2 * MODES * kt, LANES)],
        out_specs=(wide_spec,) * 4 + (gain_spec, mode_spec, mode_spec),
        compiler_params=pltpu.CompilerParams(vmem_limit_bytes=56 * 2**20),
    )(stream, key_gate, query_gate, grad_output, conv, sig, inv, inner, gain, res, lrate, ggain, gmode)
    return out, gstream, gkey, gquery, ggain.reshape(channels), gres.T, grate.T


def solution(mesh):
    wide = P("ctx", "ch")
    thin = P("ch", None)
    return jax.shard_map(
        functools.partial(local, mesh.shape["ctx"], mesh.shape["ch"]),
        mesh=mesh,
        in_specs=(wide, wide, wide, wide, P("ch"), thin, thin),
        out_specs=(wide, wide, wide, wide, P("ch"), thin, thin),
        check_vma=False,
    )
```

```python
import functools
import math

import jax
import jax.numpy as jnp
from jax import lax
from jax.experimental import pallas as pl
from jax.experimental.pallas import tpu as pltpu
from jax.sharding import PartitionSpec as P

D = 4096
MODES = 16
epsilon = 1e-05
LANES = 128
RB = 16
UNROLL = 8
GROUP = 8
MESH = pl.DeviceIdType.MESH
F32 = jnp.float32


def kernel(
    n, nch, rows, kt,
    stream_in, key_in, query_in, gout_in, gain, res_in, lrate_in,
    out_out, gstream_out, gkey_out, gquery_out, ggain, gmode,
    stream, key, query, gout, out, gstream, gkey, gquery, xs, gs, ys, ss, qbuf, res, lrate, apow, alen,
    col, inv_col, nrm_buf, inner_buf, io_s,
    sbuf, tbuf, state, part, rsbuf, agbuf, gainbuf,
    nrm_s, nrm_r, inner_s, inner_r, s_s, s_r, t_s, t_r, rs_s, rs_r, ag_s, ag_r, gn_s, gn_r,
):
    me = lax.axis_index("ctx")
    mc = lax.axis_index("ch")
    nblk = rows // RB
    nstep = rows // UNROLL
    per = 2 * MODES // n

    def each(count, test, fn):
        def body(j, carry):
            @pl.when(test(j))
            def _():
                fn(j)

            return carry

        lax.fori_loop(0, count, body, 0)

    def remote(src, dst, ssem, rsem, axis, j):
        return pltpu.make_async_remote_copy(
            src_ref=src, dst_ref=dst, send_sem=ssem, recv_sem=rsem,
            device_id={axis: j}, device_id_type=MESH,
        )

    def c_nrm(j):
        return remote(nrm_buf.at[mc], nrm_buf.at[mc], nrm_s.at[j], nrm_r.at[mc], "ch", j)

    def w_nrm(j):
        return remote(nrm_buf.at[j], nrm_buf.at[j], nrm_s.at[j], nrm_r.at[j], "ch", j)

    def c_inner(j):
        return remote(inner_buf.at[mc], inner_buf.at[mc], inner_s.at[j], inner_r.at[mc], "ch", j)

    def w_inner(j):
        return remote(inner_buf.at[j], inner_buf.at[j], inner_s.at[j], inner_r.at[j], "ch", j)

    def c_s(j):
        return remote(sbuf.at[me], sbuf.at[me], s_s.at[j], s_r.at[me], "ctx", j)

    def w_s(j):
        return remote(sbuf.at[j], sbuf.at[j], s_s.at[j], s_r.at[j], "ctx", j)

    def c_t(j):
        return remote(tbuf.at[me], tbuf.at[me], t_s.at[j], t_r.at[me], "ctx", j)

    def w_t(j):
        return remote(tbuf.at[j], tbuf.at[j], t_s.at[j], t_r.at[j], "ctx", j)

    def c_rs(j):
        return remote(part.at[pl.ds(j * per, per)], rsbuf.at[me], rs_s.at[j], rs_r.at[me], "ctx", j)

    def w_rs(j):
        return remote(rsbuf.at[j], rsbuf.at[j], rs_s.at[j], rs_r.at[j], "ctx", j)

    def c_ag(j):
        return remote(agbuf.at[me], agbuf.at[me], ag_s.at[j], ag_r.at[me], "ctx", j)

    def w_ag(j):
        return remote(agbuf.at[j], agbuf.at[j], ag_s.at[j], ag_r.at[j], "ctx", j)

    def c_gn(j):
        return remote(gainbuf.at[me], gainbuf.at[me], gn_s.at[j], gn_r.at[me], "ctx", j)

    def w_gn(j):
        return remote(gainbuf.at[j], gainbuf.at[j], gn_s.at[j], gn_r.at[j], "ctx", j)

    reads = [
        pltpu.make_async_copy(src, dst, io_s.at[i])
        for i, (src, dst) in enumerate(
            ((stream_in, stream), (gout_in, gout), (query_in, query), (key_in, key))
        )
    ]
    for copy in reads:
        copy.start()
    writes = [
        pltpu.make_async_copy(src, dst, io_s.at[4 + i])
        for i, (src, dst) in enumerate(((gkey, gkey_out), (out, out_out), (gquery, gquery_out), (gstream, gstream_out)))
    ]

    barrier = pltpu.get_barrier_semaphore()
    each(n, lambda j: j != me, lambda j: pl.semaphore_signal(
        barrier, inc=1, device_id={"ctx": j}, device_id_type=MESH))
    each(nch, lambda j: j != mc, lambda j: pl.semaphore_signal(
        barrier, inc=1, device_id={"ch": j}, device_id_type=MESH))

    for k in range(kt):
        mode_rows = pl.ds(k, MODES, stride=kt)
        res[mode_rows, :] = res_in[:, k * LANES : (k + 1) * LANES]
        lrate[mode_rows, :] = lrate_in[:, k * LANES : (k + 1) * LANES]
    rate = jnp.exp(lrate[...])
    apow[...] = jnp.exp(-rate)
    alen[...] = jnp.exp(-rate * float(rows))

    def lanes(k):
        return pl.ds(k * LANES, LANES)

    def rows_of(b):
        return pl.ds(pl.multiple_of(b * RB, RB), RB)

    def spread(b, k):
        return pl.ds(b * (RB * kt) + k, RB, stride=kt)

    def at(t):
        return pl.ds(pl.multiple_of(t * kt, kt), kt)

    def to_row(ref):
        return jnp.broadcast_to(jnp.sum(ref[...].T, axis=0, keepdims=True), (8, rows))

    def first(b, carry):
        r = rows_of(b)
        total = jnp.zeros((RB, LANES), F32)
        for k in range(kt):
            s = stream[r, lanes(k)].astype(F32)
            total += s * s
        col[r, :] = total
        return carry

    reads[0].wait()
    lax.fori_loop(0, nblk, first, 0)
    nrm_buf[mc] = to_row(col)
    pl.semaphore_wait(barrier, n - 1 + nch - 1)
    each(nch, lambda j: j != mc, lambda j: c_nrm(j).start())

    def cotangent(b, carry):
        r = rows_of(b)
        for k in range(kt):
            gs[spread(b, k), :] = gout[r, lanes(k)].astype(F32) * query[r, lanes(k)].astype(F32)
        return carry

    reads[1].wait()
    reads[2].wait()
    lax.fori_loop(0, nblk, cotangent, 0)

    def mode(ref, m):
        return ref[m * kt : (m + 1) * kt, :]

    def tree(terms):
        while len(terms) > 1:
            terms = [sum(terms[i + 1 : i + 2], terms[i]) for i in range(0, len(terms), 2)]
        return terms[0]

    def end_state(src, backward):
        a = [mode(apow, m) for m in range(MODES)]

        def body(i, carry):
            h = list(carry)
            for u in range(UNROLL):
                t = i * UNROLL + u
                x = src[at(rows - 1 - t if backward else t), :]
                for m in range(MODES):
                    h[m] = a[m] * h[m] + x
            return tuple(h)

        zero = jnp.zeros((kt, LANES), F32)
        return lax.fori_loop(0, nstep, body, (zero,) * MODES)

    ends = end_state(gs, True)
    for m in range(MODES):
        tbuf[me, m * kt : (m + 1) * kt, :] = ends[m]
    each(n, lambda j: j < me, lambda j: c_t(j).start())

    each(nch, lambda j: j != mc, lambda j: w_nrm(j).wait_recv())
    total = nrm_buf[0]
    for j in range(1, nch):
        total = total + nrm_buf[j]
    inv_row = lax.rsqrt(total / D + epsilon)
    inv_col[...] = jnp.broadcast_to(inv_row[0:1], (LANES, rows)).T
    reads[3].wait()

    def second(b, carry):
        r = rows_of(b)
        iv = inv_col[r, :]
        for k in range(kt):
            normed = stream[r, lanes(k)].astype(F32) * iv * gain[k : k + 1, :]
            x = (key[r, lanes(k)].astype(F32) * normed).astype(jnp.bfloat16)
            xs[spread(b, k), :] = x.astype(F32)
        return carry

    lax.fori_loop(0, nblk, second, 0)
    ends = end_state(xs, False)
    for m in range(MODES):
        sbuf[me, m * kt : (m + 1) * kt, :] = ends[m]
    each(n, lambda j: j > me, lambda j: c_s(j).start())

    def backward(group):
        m0 = group * GROUP
        a = [mode(apow, m0 + m) for m in range(GROUP)]
        c = [mode(res, m0 + m) for m in range(GROUP)]

        def body(i, carry):
            q = list(carry)
            for u in range(UNROLL):
                t = rows - 1 - (i * UNROLL + u)
                g = gs[at(t), :]
                terms = [ss[at(t), :]] if group else []
                for m in range(GROUP):
                    q[m] = a[m] * q[m] + g
                    qbuf[t, m0 + m] = q[m]
                    terms.append(c[m] * q[m])
                ss[at(t), :] = tree(terms)
            return tuple(q)

        lax.fori_loop(0, nstep, body, tuple(mode(state.at[1], m0 + m) for m in range(GROUP)))

    def forward(group):
        m0 = group * GROUP
        a = [mode(apow, m0 + m) for m in range(GROUP)]
        c = [mode(res, m0 + m) for m in range(GROUP)]
        zero = jnp.zeros((kt, LANES), F32)

        def body(i, carry):
            h, gr, gw = (list(v) for v in carry)
            for u in range(UNROLL):
                t = i * UNROLL + u
                x = xs[at(t), :]
                g = gs[at(t), :]
                terms = [ys[at(t), :]] if group else []
                for m in range(GROUP):
                    z = a[m] * h[m]
                    gw[m] = gw[m] + z * qbuf[t, m0 + m]
                    h[m] = z + x
                    gr[m] = gr[m] + g * h[m]
                    terms.append(c[m] * h[m])
                ys[at(t), :] = tree(terms)
            return tuple(h), tuple(gr), tuple(gw)

        start = tuple(mode(state.at[0], m0 + m) for m in range(GROUP))
        unused, gr, gw = lax.fori_loop(0, nstep, body, (start, (zero,) * GROUP, (zero,) * GROUP))
        for m in range(GROUP):
            part[m0 + m] = gr[m]
            part[MODES + m0 + m] = gw[m]

    state[...] = jnp.zeros_like(state)

    def take_t(i):
        j = n - 1 - i
        w_t(j).wait_recv()
        state[1] = alen[...] * state[1] + tbuf[j]

    each(n, lambda i: n - 1 - i > me, take_t)
    for group in range(MODES // GROUP):
        backward(group)

    def take_s(j):
        w_s(j).wait_recv()
        state[0] = alen[...] * state[0] + sbuf[j]

    each(n, lambda j: j < me, take_s)
    for group in range(MODES // GROUP):
        forward(group)
    rsbuf[me] = part[pl.ds(me * per, per)]
    each(n, lambda j: j != me, lambda j: c_rs(j).start())

    def third(b, carry):
        r = rows_of(b)
        iv = inv_col[r, :]
        total = jnp.zeros((RB, LANES), F32)
        gains = list(carry)
        for k in range(kt):
            unit = stream[r, lanes(k)].astype(F32) * iv
            sig = ss[spread(b, k), :]
            gk = gain[k : k + 1, :]
            gkey[r, lanes(k)] = (sig * (unit * gk)).astype(jnp.bfloat16)
            prod = sig * key[r, lanes(k)].astype(F32) * unit
            gains[k] = gains[k] + prod
            total += prod * gk
        col[r, :] = total
        return tuple(gains)

    gains = lax.fori_loop(0, nblk, third, (jnp.zeros((RB, LANES), F32),) * kt)
    inner_buf[mc] = to_row(col)
    each(nch, lambda j: j != mc, lambda j: c_inner(j).start())
    for k in range(kt):
        gainbuf[me, k : k + 1, :] = jnp.sum(gains[k], axis=0, keepdims=True)
    each(n, lambda j: j != me, lambda j: c_gn(j).start())
    writes[0].start()

    each(n, lambda j: j != me, lambda j: w_rs(j).wait_recv())
    agbuf[me] = lax.fori_loop(1, n, lambda j, acc: acc + rsbuf[j], rsbuf[0])
    each(n, lambda j: j != me, lambda j: c_ag(j).start())

    def fourth(b, carry):
        r = rows_of(b)
        for k in range(kt):
            conv = ys[spread(b, k), :]
            out[r, lanes(k)] = (query[r, lanes(k)].astype(F32) * conv).astype(jnp.bfloat16)
            gquery[r, lanes(k)] = (gout[r, lanes(k)].astype(F32) * conv).astype(jnp.bfloat16)
        return carry

    lax.fori_loop(0, nblk, fourth, 0)
    writes[1].start()
    writes[2].start()

    each(nch, lambda j: j != mc, lambda j: w_inner(j).wait_recv())
    total = inner_buf[0]
    for j in range(1, nch):
        total = total + inner_buf[j]
    col[...] = jnp.broadcast_to((total / D)[0:1], (LANES, rows)).T

    def fifth(b, carry):
        r = rows_of(b)
        iv = inv_col[r, :]
        mean = col[r, :]
        for k in range(kt):
            unit = stream[r, lanes(k)].astype(F32) * iv
            unit_grad = ss[spread(b, k), :] * key[r, lanes(k)].astype(F32) * gain[k : k + 1, :]
            gstream[r, lanes(k)] = (iv * (unit_grad - unit * mean)).astype(jnp.bfloat16)
        return carry

    lax.fori_loop(0, nblk, fifth, 0)
    writes[3].start()

    scale = 1.0 / math.sqrt(rows * n)
    each(n, lambda j: j != me, lambda j: w_gn(j).wait_recv())
    ggain[...] = lax.fori_loop(1, n, lambda j, acc: acc + gainbuf[j], gainbuf[0]) * scale
    each(n, lambda j: j != me, lambda j: w_ag(j).wait_recv())
    for m in range(2 * MODES):
        gmode[m * kt : (m + 1) * kt, :] = agbuf[m // per, m % per] * scale

    each(nch, lambda j: j != mc, lambda j: c_nrm(j).wait_send())
    each(nch, lambda j: j != mc, lambda j: c_inner(j).wait_send())
    each(n, lambda j: j < me, lambda j: c_t(j).wait_send())
    each(n, lambda j: j > me, lambda j: c_s(j).wait_send())
    each(n, lambda j: j != me, lambda j: c_gn(j).wait_send())
    each(n, lambda j: j != me, lambda j: c_rs(j).wait_send())
    each(n, lambda j: j != me, lambda j: c_ag(j).wait_send())
    for copy in writes:
        copy.wait()


def finish(
    kt, parts,
    a_in, b_in, c_in, d_in, res, lrate, ggain_in, gmode,
    a_out, b_out, c_out, d_out, ggain, gres, grate,
    a, b, c, d, read_s, write_s,
):
    height = a.shape[0] // parts
    moves = []
    for i in range(parts):
        r = pl.ds(i * height, height)
        for j, (src, held, dst) in enumerate(
            ((a_in, a, a_out), (b_in, b, b_out), (c_in, c, c_out), (d_in, d, d_out))
        ):
            at = i * 4 + j
            moves.append((
                pltpu.make_async_copy(src.at[r], held.at[r], read_s.at[at]),
                pltpu.make_async_copy(held.at[r], dst.at[r], write_s.at[at]),
            ))
    for read, write in moves:
        read.start()
    ggain[...] = ggain_in[...]
    for k in range(kt):
        cols = slice(k * LANES, (k + 1) * LANES)
        gres[:, cols] = gmode[pl.ds(k, MODES, stride=kt), :]
        weighted = gmode[pl.ds(MODES * kt + k, MODES, stride=kt), :]
        grate[:, cols] = -jnp.exp(lrate[:, cols]) * res[:, cols] * weighted
    for read, write in moves:
        read.wait()
        write.start()
    for read, write in moves:
        write.wait()


def local(n, nch, stream, key_gate, query_gate, grad_output, norm_gain, residue, log_rate):
    rows, channels = stream.shape
    kt = channels // LANES
    per = 2 * MODES // n
    vm = pl.BlockSpec(memory_space=pltpu.VMEM)
    anywhere = pl.BlockSpec(memory_space=pl.ANY)
    wide = jax.ShapeDtypeStruct((rows, channels), jnp.bfloat16)
    gain_out = jax.ShapeDtypeStruct((kt, LANES), F32)
    mode_out = jax.ShapeDtypeStruct((2 * MODES * kt, LANES), F32)
    dma = pltpu.SemaphoreType.DMA
    held = pltpu.VMEM((rows, channels), jnp.bfloat16)
    flat = pltpu.VMEM((rows * kt, LANES), F32)
    one = pltpu.VMEM((rows, LANES), F32)
    lined = pltpu.VMEM((nch, 8, rows), F32)
    ends = pltpu.VMEM((n, MODES * kt, LANES), F32)
    modal = pltpu.VMEM((MODES * kt, LANES), F32)
    pieces = pltpu.VMEM((n, per, kt, LANES), F32)
    gain = norm_gain.reshape(kt, LANES)
    res, lrate = residue.T, log_rate.T
    out, gstream, gkey, gquery, ggain, gmode = pl.pallas_call(
        functools.partial(kernel, n, nch, rows, kt),
        out_shape=(wide, wide, wide, wide, gain_out, mode_out),
        in_specs=[anywhere] * 4 + [vm] * 3,
        out_specs=(anywhere,) * 4 + (vm,) * 2,
        scratch_shapes=[
            held, held, held, held, held, held, held, held,
            flat, flat, flat, flat,
            pltpu.VMEM((rows, MODES, kt, LANES), F32),
            modal, modal, modal, modal, one, one,
            lined, lined, dma((8,)), ends, ends,
            pltpu.VMEM((2, MODES * kt, LANES), F32),
            pltpu.VMEM((2 * MODES, kt, LANES), F32),
            pieces, pieces,
            pltpu.VMEM((n, kt, LANES), F32),
            dma((nch,)), dma((nch,)), dma((nch,)), dma((nch,)),
        ] + [dma((n,))] * 10,
        compiler_params=pltpu.CompilerParams(
            collective_id=0, has_side_effects=True, vmem_limit_bytes=56 * 2**20
        ),
    )(stream, key_gate, query_gate, grad_output, gain, res, lrate)

    parts = 4
    mode_t = jax.ShapeDtypeStruct((MODES, channels), F32)
    out, gstream, gkey, gquery, ggain, gres, grate = pl.pallas_call(
        functools.partial(finish, kt, parts),
        out_shape=(wide, wide, wide, wide, gain_out, mode_t, mode_t),
        in_specs=[anywhere] * 4 + [vm] * 4,
        out_specs=(anywhere,) * 4 + (vm,) * 3,
        scratch_shapes=[held, held, held, held, dma((4 * parts,)), dma((4 * parts,))],
        compiler_params=pltpu.CompilerParams(vmem_limit_bytes=56 * 2**20),
    )(out, gstream, gkey, gquery, res, lrate, ggain, gmode)
    return out, gstream, gkey, gquery, ggain.reshape(channels), gres.T, grate.T


def solution(mesh):
    wide = P("ctx", "ch")
    thin = P("ch", None)
    return jax.shard_map(
        functools.partial(local, mesh.shape["ctx"], mesh.shape["ch"]),
        mesh=mesh,
        in_specs=(wide, wide, wide, wide, P("ch"), thin, thin),
        out_specs=(wide, wide, wide, wide, P("ch"), thin, thin),
        check_vma=False,
    )
```

```python
import functools
import math

import jax
import jax.numpy as jnp
from jax import lax
from jax.experimental import pallas as pl
from jax.experimental.pallas import tpu as pltpu
from jax.sharding import PartitionSpec as P

D = 4096
MODES = 16
epsilon = 1e-05
LANES = 128
RB = 16
UNROLL = 16
GROUP = 8
MESH = pl.DeviceIdType.MESH
F32 = jnp.float32


def kernel(
    n, nch, rows, kt,
    stream_in, key_in, query_in, gout_in, gain, res_in, lrate_in,
    out_out, gstream_out, gkey_out, gquery_out, ggain, gmode,
    stream, key, query, gout, out, gstream, gkey, gquery, xs, gs, ys, ss, qbuf, res, lrate, apow, alen,
    col, inv_col, nrm_buf, inner_buf, io_s,
    sbuf, tbuf, state, part, rsbuf, agbuf, gainbuf,
    nrm_s, nrm_r, inner_s, inner_r, s_s, s_r, t_s, t_r, rs_s, rs_r, ag_s, ag_r, gn_s, gn_r,
):
    me = lax.axis_index("ctx")
    mc = lax.axis_index("ch")
    nblk = rows // RB
    nstep = rows // UNROLL
    per = 2 * MODES // n

    def each(count, test, fn):
        def body(j, carry):
            @pl.when(test(j))
            def _():
                fn(j)

            return carry

        lax.fori_loop(0, count, body, 0)

    def remote(src, dst, ssem, rsem, axis, j):
        return pltpu.make_async_remote_copy(
            src_ref=src, dst_ref=dst, send_sem=ssem, recv_sem=rsem,
            device_id={axis: j}, device_id_type=MESH,
        )

    def c_nrm(j):
        return remote(nrm_buf.at[mc], nrm_buf.at[mc], nrm_s.at[j], nrm_r.at[mc], "ch", j)

    def w_nrm(j):
        return remote(nrm_buf.at[j], nrm_buf.at[j], nrm_s.at[j], nrm_r.at[j], "ch", j)

    def c_inner(j):
        return remote(inner_buf.at[mc], inner_buf.at[mc], inner_s.at[j], inner_r.at[mc], "ch", j)

    def w_inner(j):
        return remote(inner_buf.at[j], inner_buf.at[j], inner_s.at[j], inner_r.at[j], "ch", j)

    def c_s(j):
        return remote(sbuf.at[me], sbuf.at[me], s_s.at[j], s_r.at[me], "ctx", j)

    def w_s(j):
        return remote(sbuf.at[j], sbuf.at[j], s_s.at[j], s_r.at[j], "ctx", j)

    def c_t(j):
        return remote(tbuf.at[me], tbuf.at[me], t_s.at[j], t_r.at[me], "ctx", j)

    def w_t(j):
        return remote(tbuf.at[j], tbuf.at[j], t_s.at[j], t_r.at[j], "ctx", j)

    def c_rs(j):
        return remote(part.at[pl.ds(j * per, per)], rsbuf.at[me], rs_s.at[j], rs_r.at[me], "ctx", j)

    def w_rs(j):
        return remote(rsbuf.at[j], rsbuf.at[j], rs_s.at[j], rs_r.at[j], "ctx", j)

    def c_ag(j):
        return remote(agbuf.at[me], agbuf.at[me], ag_s.at[j], ag_r.at[me], "ctx", j)

    def w_ag(j):
        return remote(agbuf.at[j], agbuf.at[j], ag_s.at[j], ag_r.at[j], "ctx", j)

    def c_gn(j):
        return remote(gainbuf.at[me], gainbuf.at[me], gn_s.at[j], gn_r.at[me], "ctx", j)

    def w_gn(j):
        return remote(gainbuf.at[j], gainbuf.at[j], gn_s.at[j], gn_r.at[j], "ctx", j)

    reads = [
        pltpu.make_async_copy(src, dst, io_s.at[i])
        for i, (src, dst) in enumerate(
            ((stream_in, stream), (gout_in, gout), (query_in, query), (key_in, key))
        )
    ]
    for copy in reads:
        copy.start()
    writes = [
        pltpu.make_async_copy(src, dst, io_s.at[4 + i])
        for i, (src, dst) in enumerate(((gkey, gkey_out), (out, out_out), (gquery, gquery_out), (gstream, gstream_out)))
    ]

    barrier = pltpu.get_barrier_semaphore()
    each(n, lambda j: j != me, lambda j: pl.semaphore_signal(
        barrier, inc=1, device_id={"ctx": j}, device_id_type=MESH))
    each(nch, lambda j: j != mc, lambda j: pl.semaphore_signal(
        barrier, inc=1, device_id={"ch": j}, device_id_type=MESH))

    for k in range(kt):
        mode_rows = pl.ds(k, MODES, stride=kt)
        res[mode_rows, :] = res_in[:, k * LANES : (k + 1) * LANES]
        lrate[mode_rows, :] = lrate_in[:, k * LANES : (k + 1) * LANES]
    rate = jnp.exp(lrate[...])
    apow[...] = jnp.exp(-rate)
    alen[...] = jnp.exp(-rate * float(rows))

    def lanes(k):
        return pl.ds(k * LANES, LANES)

    def rows_of(b):
        return pl.ds(pl.multiple_of(b * RB, RB), RB)

    def spread(b, k):
        return pl.ds(b * (RB * kt) + k, RB, stride=kt)

    def at(t):
        return pl.ds(pl.multiple_of(t * kt, kt), kt)

    def to_row(ref):
        return jnp.broadcast_to(jnp.sum(ref[...].T, axis=0, keepdims=True), (8, rows))

    def first(b, carry):
        r = rows_of(b)
        total = jnp.zeros((RB, LANES), F32)
        for k in range(kt):
            s = stream[r, lanes(k)].astype(F32)
            total += s * s
        col[r, :] = total
        return carry

    reads[0].wait()
    lax.fori_loop(0, nblk, first, 0)
    nrm_buf[mc] = to_row(col)
    pl.semaphore_wait(barrier, n - 1 + nch - 1)
    each(nch, lambda j: j != mc, lambda j: c_nrm(j).start())

    def cotangent(b, carry):
        r = rows_of(b)
        for k in range(kt):
            gs[spread(b, k), :] = gout[r, lanes(k)].astype(F32) * query[r, lanes(k)].astype(F32)
        return carry

    reads[1].wait()
    reads[2].wait()
    lax.fori_loop(0, nblk, cotangent, 0)

    def mode(ref, m):
        return ref[m * kt : (m + 1) * kt, :]

    def tree(terms):
        while len(terms) > 1:
            terms = [sum(terms[i + 1 : i + 2], terms[i]) for i in range(0, len(terms), 2)]
        return terms[0]

    def end_state(src, backward):
        a = [mode(apow, m) for m in range(MODES)]

        def body(i, carry):
            h = list(carry)
            for u in range(UNROLL):
                t = i * UNROLL + u
                x = src[at(rows - 1 - t if backward else t), :]
                for m in range(MODES):
                    h[m] = a[m] * h[m] + x
            return tuple(h)

        zero = jnp.zeros((kt, LANES), F32)
        return lax.fori_loop(0, nstep, body, (zero,) * MODES)

    ends = end_state(gs, True)
    for m in range(MODES):
        tbuf[me, m * kt : (m + 1) * kt, :] = ends[m]
    each(n, lambda j: j < me, lambda j: c_t(j).start())

    each(nch, lambda j: j != mc, lambda j: w_nrm(j).wait_recv())
    total = nrm_buf[0]
    for j in range(1, nch):
        total = total + nrm_buf[j]
    inv_row = lax.rsqrt(total / D + epsilon)
    inv_col[...] = jnp.broadcast_to(inv_row[0:1], (LANES, rows)).T
    reads[3].wait()

    def second(b, carry):
        r = rows_of(b)
        iv = inv_col[r, :]
        for k in range(kt):
            normed = stream[r, lanes(k)].astype(F32) * iv * gain[k : k + 1, :]
            x = (key[r, lanes(k)].astype(F32) * normed).astype(jnp.bfloat16)
            xs[spread(b, k), :] = x.astype(F32)
        return carry

    lax.fori_loop(0, nblk, second, 0)
    ends = end_state(xs, False)
    for m in range(MODES):
        sbuf[me, m * kt : (m + 1) * kt, :] = ends[m]
    each(n, lambda j: j > me, lambda j: c_s(j).start())

    def backward(group):
        m0 = group * GROUP
        a = [mode(apow, m0 + m) for m in range(GROUP)]
        c = [mode(res, m0 + m) for m in range(GROUP)]

        def body(i, carry):
            q = list(carry)
            for u in range(UNROLL):
                t = rows - 1 - (i * UNROLL + u)
                g = gs[at(t), :]
                terms = [ss[at(t), :]] if group else []
                for m in range(GROUP):
                    q[m] = a[m] * q[m] + g
                    qbuf[t, m0 + m] = q[m]
                    terms.append(c[m] * q[m])
                ss[at(t), :] = tree(terms)
            return tuple(q)

        lax.fori_loop(0, nstep, body, tuple(mode(state.at[1], m0 + m) for m in range(GROUP)))

    def forward(group):
        m0 = group * GROUP
        a = [mode(apow, m0 + m) for m in range(GROUP)]
        c = [mode(res, m0 + m) for m in range(GROUP)]
        zero = jnp.zeros((kt, LANES), F32)

        def body(i, carry):
            h, gr, gw = (list(v) for v in carry)
            for u in range(UNROLL):
                t = i * UNROLL + u
                x = xs[at(t), :]
                g = gs[at(t), :]
                terms = [ys[at(t), :]] if group else []
                for m in range(GROUP):
                    z = a[m] * h[m]
                    gw[m] = gw[m] + z * qbuf[t, m0 + m]
                    h[m] = z + x
                    gr[m] = gr[m] + g * h[m]
                    terms.append(c[m] * h[m])
                ys[at(t), :] = tree(terms)
            return tuple(h), tuple(gr), tuple(gw)

        start = tuple(mode(state.at[0], m0 + m) for m in range(GROUP))
        unused, gr, gw = lax.fori_loop(0, nstep, body, (start, (zero,) * GROUP, (zero,) * GROUP))
        for m in range(GROUP):
            part[m0 + m] = gr[m]
            part[MODES + m0 + m] = gw[m]

    state[...] = jnp.zeros_like(state)

    def take_t(i):
        j = n - 1 - i
        w_t(j).wait_recv()
        state[1] = alen[...] * state[1] + tbuf[j]

    each(n, lambda i: n - 1 - i > me, take_t)
    for group in range(MODES // GROUP):
        backward(group)

    def take_s(j):
        w_s(j).wait_recv()
        state[0] = alen[...] * state[0] + sbuf[j]

    each(n, lambda j: j < me, take_s)
    for group in range(MODES // GROUP):
        forward(group)
    rsbuf[me] = part[pl.ds(me * per, per)]
    each(n, lambda j: j != me, lambda j: c_rs(j).start())

    def third(b, carry):
        r = rows_of(b)
        iv = inv_col[r, :]
        total = jnp.zeros((RB, LANES), F32)
        gains = list(carry)
        for k in range(kt):
            unit = stream[r, lanes(k)].astype(F32) * iv
            sig = ss[spread(b, k), :]
            gk = gain[k : k + 1, :]
            gkey[r, lanes(k)] = (sig * (unit * gk)).astype(jnp.bfloat16)
            prod = sig * key[r, lanes(k)].astype(F32) * unit
            gains[k] = gains[k] + prod
            total += prod * gk
        col[r, :] = total
        return tuple(gains)

    gains = lax.fori_loop(0, nblk, third, (jnp.zeros((RB, LANES), F32),) * kt)
    inner_buf[mc] = to_row(col)
    each(nch, lambda j: j != mc, lambda j: c_inner(j).start())
    for k in range(kt):
        gainbuf[me, k : k + 1, :] = jnp.sum(gains[k], axis=0, keepdims=True)
    each(n, lambda j: j != me, lambda j: c_gn(j).start())
    writes[0].start()

    each(n, lambda j: j != me, lambda j: w_rs(j).wait_recv())
    agbuf[me] = lax.fori_loop(1, n, lambda j, acc: acc + rsbuf[j], rsbuf[0])
    each(n, lambda j: j != me, lambda j: c_ag(j).start())

    def fourth(b, carry):
        r = rows_of(b)
        for k in range(kt):
            conv = ys[spread(b, k), :]
            out[r, lanes(k)] = (query[r, lanes(k)].astype(F32) * conv).astype(jnp.bfloat16)
            gquery[r, lanes(k)] = (gout[r, lanes(k)].astype(F32) * conv).astype(jnp.bfloat16)
        return carry

    lax.fori_loop(0, nblk, fourth, 0)
    writes[1].start()
    writes[2].start()

    each(nch, lambda j: j != mc, lambda j: w_inner(j).wait_recv())
    total = inner_buf[0]
    for j in range(1, nch):
        total = total + inner_buf[j]
    col[...] = jnp.broadcast_to((total / D)[0:1], (LANES, rows)).T

    def fifth(b, carry):
        r = rows_of(b)
        iv = inv_col[r, :]
        mean = col[r, :]
        for k in range(kt):
            unit = stream[r, lanes(k)].astype(F32) * iv
            unit_grad = ss[spread(b, k), :] * key[r, lanes(k)].astype(F32) * gain[k : k + 1, :]
            gstream[r, lanes(k)] = (iv * (unit_grad - unit * mean)).astype(jnp.bfloat16)
        return carry

    lax.fori_loop(0, nblk, fifth, 0)
    writes[3].start()

    scale = 1.0 / math.sqrt(rows * n)
    each(n, lambda j: j != me, lambda j: w_gn(j).wait_recv())
    ggain[...] = lax.fori_loop(1, n, lambda j, acc: acc + gainbuf[j], gainbuf[0]) * scale
    each(n, lambda j: j != me, lambda j: w_ag(j).wait_recv())
    for m in range(2 * MODES):
        gmode[m * kt : (m + 1) * kt, :] = agbuf[m // per, m % per] * scale

    each(nch, lambda j: j != mc, lambda j: c_nrm(j).wait_send())
    each(nch, lambda j: j != mc, lambda j: c_inner(j).wait_send())
    each(n, lambda j: j < me, lambda j: c_t(j).wait_send())
    each(n, lambda j: j > me, lambda j: c_s(j).wait_send())
    each(n, lambda j: j != me, lambda j: c_gn(j).wait_send())
    each(n, lambda j: j != me, lambda j: c_rs(j).wait_send())
    each(n, lambda j: j != me, lambda j: c_ag(j).wait_send())
    for copy in writes:
        copy.wait()


def finish(
    kt, parts,
    a_in, b_in, c_in, d_in, res, lrate, ggain_in, gmode,
    a_out, b_out, c_out, d_out, ggain, gres, grate,
    a, b, c, d, read_s, write_s,
):
    height = a.shape[0] // parts
    moves = []
    for i in range(parts):
        r = pl.ds(i * height, height)
        for j, (src, held, dst) in enumerate(
            ((a_in, a, a_out), (b_in, b, b_out), (c_in, c, c_out), (d_in, d, d_out))
        ):
            at = i * 4 + j
            moves.append((
                pltpu.make_async_copy(src.at[r], held.at[r], read_s.at[at]),
                pltpu.make_async_copy(held.at[r], dst.at[r], write_s.at[at]),
            ))
    for read, write in moves:
        read.start()
    ggain[...] = ggain_in[...]
    for k in range(kt):
        cols = slice(k * LANES, (k + 1) * LANES)
        gres[:, cols] = gmode[pl.ds(k, MODES, stride=kt), :]
        weighted = gmode[pl.ds(MODES * kt + k, MODES, stride=kt), :]
        grate[:, cols] = -jnp.exp(lrate[:, cols]) * res[:, cols] * weighted
    for read, write in moves:
        read.wait()
        write.start()
    for read, write in moves:
        write.wait()


def local(n, nch, stream, key_gate, query_gate, grad_output, norm_gain, residue, log_rate):
    rows, channels = stream.shape
    kt = channels // LANES
    per = 2 * MODES // n
    vm = pl.BlockSpec(memory_space=pltpu.VMEM)
    anywhere = pl.BlockSpec(memory_space=pl.ANY)
    wide = jax.ShapeDtypeStruct((rows, channels), jnp.bfloat16)
    gain_out = jax.ShapeDtypeStruct((kt, LANES), F32)
    mode_out = jax.ShapeDtypeStruct((2 * MODES * kt, LANES), F32)
    dma = pltpu.SemaphoreType.DMA
    held = pltpu.VMEM((rows, channels), jnp.bfloat16)
    flat = pltpu.VMEM((rows * kt, LANES), F32)
    one = pltpu.VMEM((rows, LANES), F32)
    lined = pltpu.VMEM((nch, 8, rows), F32)
    ends = pltpu.VMEM((n, MODES * kt, LANES), F32)
    modal = pltpu.VMEM((MODES * kt, LANES), F32)
    pieces = pltpu.VMEM((n, per, kt, LANES), F32)
    gain = norm_gain.reshape(kt, LANES)
    res, lrate = residue.T, log_rate.T
    out, gstream, gkey, gquery, ggain, gmode = pl.pallas_call(
        functools.partial(kernel, n, nch, rows, kt),
        out_shape=(wide, wide, wide, wide, gain_out, mode_out),
        in_specs=[anywhere] * 4 + [vm] * 3,
        out_specs=(anywhere,) * 4 + (vm,) * 2,
        scratch_shapes=[
            held, held, held, held, held, held, held, held,
            flat, flat, flat, flat,
            pltpu.VMEM((rows, MODES, kt, LANES), F32),
            modal, modal, modal, modal, one, one,
            lined, lined, dma((8,)), ends, ends,
            pltpu.VMEM((2, MODES * kt, LANES), F32),
            pltpu.VMEM((2 * MODES, kt, LANES), F32),
            pieces, pieces,
            pltpu.VMEM((n, kt, LANES), F32),
            dma((nch,)), dma((nch,)), dma((nch,)), dma((nch,)),
        ] + [dma((n,))] * 10,
        compiler_params=pltpu.CompilerParams(
            collective_id=0, has_side_effects=True, vmem_limit_bytes=56 * 2**20
        ),
    )(stream, key_gate, query_gate, grad_output, gain, res, lrate)

    parts = 4
    mode_t = jax.ShapeDtypeStruct((MODES, channels), F32)
    out, gstream, gkey, gquery, ggain, gres, grate = pl.pallas_call(
        functools.partial(finish, kt, parts),
        out_shape=(wide, wide, wide, wide, gain_out, mode_t, mode_t),
        in_specs=[anywhere] * 4 + [vm] * 4,
        out_specs=(anywhere,) * 4 + (vm,) * 3,
        scratch_shapes=[held, held, held, held, dma((4 * parts,)), dma((4 * parts,))],
        compiler_params=pltpu.CompilerParams(vmem_limit_bytes=56 * 2**20),
    )(out, gstream, gkey, gquery, res, lrate, ggain, gmode)
    return out, gstream, gkey, gquery, ggain.reshape(channels), gres.T, grate.T


def solution(mesh):
    wide = P("ctx", "ch")
    thin = P("ch", None)
    return jax.shard_map(
        functools.partial(local, mesh.shape["ctx"], mesh.shape["ch"]),
        mesh=mesh,
        in_specs=(wide, wide, wide, wide, P("ch"), thin, thin),
        out_specs=(wide, wide, wide, wide, P("ch"), thin, thin),
        check_vma=False,
    )
```
